32 devices in a mesh: dp: 4 (over y, core), pipe: 2 (over x), tensor: 4 (over z).
Axes of the slice: x: 2, y: 2, z: 4, core: 2. Of those that a mesh axis runs over, the one named last changes fastest.
Arguments:
- hidden: bfloat16 [1536, 2048], P(('dp', 'pipe'), 'tensor'), parts along dimension 0, may hold values from -20 to 20
- weight: bfloat16 [2048, 9216], P(None, ('pipe', 'tensor')), may hold values from -16 to 16
- targets: int32 [1536], P('dp'), parts along dimension 0, may hold values from 0 to 9215
- row_weight: float32 [1536], P('dp'), parts along dimension 0, may hold values from 2 to 20
Outputs:
- grad_hidden: bfloat16 [1536, 2048], P(('dp', 'pipe'), 'tensor'), parts along dimension 0
- row_loss: float32 [1536], P('dp'), parts along dimension 0
The draws below stay inside these ranges and needn't reach their ends.
There are 4 independent parts, one for each index of `dp`. The reference program is written for one: setup_inputs(seed, part) draws one part's arguments, and reference() takes and returns one part's arrays. A program takes and returns all parts, laid end to end along the dimension named above; an argument that names none is the same for every part. Nothing has to cross between parts.
All inputs are finite; a program needn't handle non-finite values.
Results may differ from the reference program's by a relative error of at most 0.0051.
Values may be sent and summed in bfloat16 or wider, within the bound.
No kernel may reach another device: no remote copies, remote signals or barrier semaphores. Data moves between devices by JAX's collectives and lax.ppermute only.
A program may use at most 64 MiB of HBM per device.

```python
import math
import jax
import jax.numpy as jnp
from jax import lax

D = 2048
ROWS = 384
VOCAB = 9216


def draw_hidden(key, part):
    first_key = jax.random.fold_in(key, 0)
    values = jnp.clip(jax.random.normal(first_key, (ROWS, D), jnp.float32), -6.0, 6.0)
    return values.astype(jnp.bfloat16)


def draw_weight(key, part):
    spread = 3.0 / math.sqrt(D)
    values = jnp.clip(jax.random.normal(key, (D, VOCAB), jnp.float32), -6.0, 6.0) * spread
    return values.astype(jnp.bfloat16)


def set_ends(result, rng, smallest, largest):
    longest = result.shape.index(max(result.shape))
    spots = []
    for shift in (0, 1):
        where = [jax.random.randint(jax.random.fold_in(rng, axis), (), 0, length) for axis, length in enumerate(result.shape)]
        where[longest] = (where[longest] + shift) % result.shape[longest]
        spots.append(tuple(where))
    return result.at[spots[0]].set(smallest).at[spots[1]].set(largest)


def setup_inputs(seed: int = 0, part: int = 0) -> dict:
    seeds = jax.random.split(jax.random.key(seed), 5)
    part_keys = jax.random.split(jax.random.fold_in(seeds[4], part), 5)
    hidden = draw_hidden(jax.random.fold_in(jax.random.fold_in(seeds[4], part), 71), part)
    weight = draw_weight(jax.random.fold_in(seeds[4], 71), part)
    targets = set_ends(jax.random.randint(part_keys[2], (ROWS,), 0, VOCAB), jax.random.fold_in(part_keys[2], 1), 0, VOCAB - 1).astype(jnp.int32)
    row_weight = jnp.clip(jnp.exp(jax.random.uniform(part_keys[3], (ROWS,), jnp.float32, math.log(2.0), math.log(20.0))), 2.0, 20.0)
    return dict(hidden=hidden, weight=weight, targets=targets, row_weight=row_weight)


def reference(hidden, weight, targets, row_weight):
    logits = jnp.dot(hidden, weight, preferred_element_type=jnp.float32)
    row_max = jnp.max(logits, axis=1)
    shifted = jnp.exp(logits - row_max[:, None])
    sum_exp = jnp.sum(shifted, axis=1)
    is_target = lax.broadcasted_iota(jnp.int32, logits.shape, 1) == targets[:, None].astype(jnp.int32)
    label_logit = jnp.sum(jnp.where(is_target, logits, jnp.zeros_like(logits)), axis=1)
    row_loss = jnp.log(sum_exp) + row_max - label_logit
    dlogits = (row_weight[:, None] * (shifted / sum_exp[:, None] - is_target.astype(logits.dtype))).astype(jnp.bfloat16)
    grad_hidden = lax.dot_general(dlogits, weight, (((1,), (1,)), ((), ())), preferred_element_type=jnp.float32)
    return grad_hidden.astype(jnp.bfloat16), row_loss
```

```python
import jax
import jax.numpy as jnp
from jax import lax
from jax.sharding import PartitionSpec as P

CHUNKS = 1


def partners(n, k):
    if n & (n - 1):
        return [(i, (i + k) % n) for i in range(n)]
    return [(i, i ^ k) for i in range(n)]


def source(me, n, k):
    if n & (n - 1):
        return lax.rem(me - k + n, n)
    return me ^ k


def target(me, n, k):
    if n & (n - 1):
        return lax.rem(me + k, n)
    return me ^ k


def merge(a, b):
    top = jnp.maximum(a[0], b[0])
    total = a[1] * jnp.exp(a[0] - top) + b[1] * jnp.exp(b[0] - top)
    return jnp.stack([top, total, a[2] + b[2]])


def per_device(hidden, weight, targets, row_weight):
    pipes, tensors = lax.axis_size("pipe"), lax.axis_size("tensor")
    px, tz = lax.axis_index("pipe"), lax.axis_index("tensor")
    rows, width = hidden.shape
    vocab_dev = weight.shape[1]
    offset = (px * tensors + tz) * vocab_dev
    bf16, f32 = jnp.bfloat16, jnp.float32

    w_in = [lax.dynamic_slice_in_dim(weight, source(tz, tensors, k) * width, width, 0) for k in range(tensors)]
    if tensors & (tensors - 1):
        w_out = [lax.dynamic_slice_in_dim(weight, target(tz, tensors, k) * width, width, 0) for k in range(tensors)]
    else:
        w_out = w_in

    def tensor_permute(a, k):
        return a if k == 0 else lax.ppermute(a, "tensor", partners(tensors, k))

    def pipe_permute(a, j):
        return a if j == 0 else lax.ppermute(a, "pipe", partners(pipes, j))

    step = rows // CHUNKS
    local_targets = [targets.reshape(pipes, rows)[source(px, pipes, j)] for j in range(pipes)]
    local_scale = [row_weight.reshape(pipes, rows)[source(px, pipes, j)] for j in range(pipes)]
    columns = lax.broadcasted_iota(jnp.int32, (step, vocab_dev), 1) + offset
    grads, losses = [], []
    for c in range(CHUNKS):
        piece = hidden[c * step : (c + 1) * step]
        arrived = [tensor_permute(piece, k) for k in range(tensors)]
        logits, stats = [], []
        for j in range(pipes):
            acc = 0
            for k in range(tensors):
                acc += jnp.dot(pipe_permute(arrived[k], j), w_in[k], preferred_element_type=f32)
            logits.append(acc)
            t = local_targets[j][c * step : (c + 1) * step]
            m = jnp.max(acc, axis=1)
            s = jnp.sum(jnp.exp(acc - m[:, None]), axis=1)
            label = jnp.sum(jnp.where(columns == t[:, None], acc, 0.0), axis=1)
            stats.append(jnp.stack([m, s, label]))
        mine = jnp.stack(stats)
        if pipes == 2:
            other = pipe_permute(mine, 1)[::-1]
            mine = jax.vmap(merge)(mine, other)
        else:
            whole = jnp.zeros_like(mine)
            for j in range(pipes):
                whole = whole.at[source(px, pipes, j)].set(mine[j])
            every = lax.all_gather(whole, "pipe")
            whole = every[0]
            for p in range(1, pipes):
                whole = jax.vmap(merge)(whole, every[p])
            mine = jnp.stack([whole[source(px, pipes, j)] for j in range(pipes)])
        total = mine
        for k in range(1, tensors):
            total = jax.vmap(merge)(total, tensor_permute(mine, k))
        dlogits = []
        loss = jnp.zeros((pipes, step), f32)
        for j in range(pipes):
            m, s, label = total[j]
            t = local_targets[j][c * step : (c + 1) * step]
            g = local_scale[j][c * step : (c + 1) * step]
            hit = (columns == t[:, None]).astype(f32)
            dlogits.append((g[:, None] * (jnp.exp(logits[j] - m[:, None]) / s[:, None] - hit)).astype(bf16))
            loss = loss.at[source(px, pipes, j)].set(jnp.log(s) + m - label)
        losses.append(loss)
        contract = (((1,), (1,)), ((), ()))
        sums = [None] * tensors
        for k in list(range(tensors - 1, -1, -1)):
            acc = 0
            for j in range(pipes - 1, -1, -1):
                part = lax.dot_general(dlogits[j], w_out[k], contract, preferred_element_type=f32)
                if j:
                    part = lax.ppermute(part.astype(bf16), "pipe", [(b, a) for a, b in partners(pipes, j)]).astype(f32)
                acc += part
            if k:
                acc = tensor_permute(acc.astype(bf16), k).astype(f32)
            sums[k] = acc
        grads.append(sum(sums[1:], sums[0]).astype(bf16))
    grad = jnp.concatenate(grads, axis=0)
    row_loss = jnp.concatenate(losses, axis=1).reshape(-1)
    return grad, row_loss


def solution(mesh):
    in_specs = (P(("dp", "pipe"), "tensor"), P(None, ("pipe", "tensor")), P("dp"), P("dp"))
    out_specs = (P(("dp", "pipe"), "tensor"), P("dp"))
    return jax.shard_map(
        per_device, mesh=mesh, in_specs=in_specs, out_specs=out_specs, check_vma=False
    )
```

```python
import jax
import jax.numpy as jnp
from jax import lax
from jax.experimental import pallas as pl
from jax.experimental.pallas import tpu as pltpu
from jax.sharding import PartitionSpec as P

BF16, F32 = jnp.bfloat16, jnp.float32
ROWS_BY_ROWS = (((1,), (1,)), ((), ()))
VMEM = pl.BlockSpec(memory_space=pltpu.VMEM)
SMEM = pl.BlockSpec(memory_space=pltpu.SMEM)
HBM = pl.BlockSpec(memory_space=pltpu.HBM)
LIMIT = pltpu.CompilerParams(vmem_limit_bytes=24 * 2**20)


def partners(n, k):
    if n & (n - 1):
        return [(i, (i + k) % n) for i in range(n)]
    return [(i, i ^ k) for i in range(n)]


def source(me, n, k):
    if n & (n - 1):
        return lax.rem(me - k + n, n)
    return me ^ k


def target(me, n, k):
    if n & (n - 1):
        return lax.rem(me + k, n)
    return me ^ k


def merge(a, b):
    top = jnp.maximum(a[0], b[0])
    total = a[1] * jnp.exp(a[0] - top) + b[1] * jnp.exp(b[0] - top)
    return jnp.stack([top, total, a[2] + b[2]])


def any_mesh(hidden, weight, targets, row_weight):
    pipes, tensors = lax.axis_size("pipe"), lax.axis_size("tensor")
    px, tz = lax.axis_index("pipe"), lax.axis_index("tensor")
    rows, width = hidden.shape
    vocab_dev = weight.shape[1]
    offset = (px * tensors + tz) * vocab_dev

    w_in = [lax.dynamic_slice_in_dim(weight, source(tz, tensors, k) * width, width, 0) for k in range(tensors)]
    w_out = [lax.dynamic_slice_in_dim(weight, target(tz, tensors, k) * width, width, 0) for k in range(tensors)]

    def tensor_permute(a, k):
        return a if k == 0 else lax.ppermute(a, "tensor", partners(tensors, k))

    def pipe_permute(a, j):
        return a if j == 0 else lax.ppermute(a, "pipe", partners(pipes, j))

    local_targets = [targets.reshape(pipes, rows)[source(px, pipes, j)] for j in range(pipes)]
    local_scale = [row_weight.reshape(pipes, rows)[source(px, pipes, j)] for j in range(pipes)]
    columns = lax.broadcasted_iota(jnp.int32, (rows, vocab_dev), 1) + offset
    arrived = [tensor_permute(hidden, k) for k in range(tensors)]
    logits, stats = [], []
    for j in range(pipes):
        acc = 0
        for k in range(tensors):
            acc += jnp.dot(pipe_permute(arrived[k], j), w_in[k], preferred_element_type=F32)
        logits.append(acc)
        m = jnp.max(acc, axis=1)
        s = jnp.sum(jnp.exp(acc - m[:, None]), axis=1)
        label = jnp.sum(jnp.where(columns == local_targets[j][:, None], acc, 0.0), axis=1)
        stats.append(jnp.stack([m, s, label]))
    mine = jnp.stack(stats)
    whole = jnp.zeros_like(mine)
    for j in range(pipes):
        whole = whole.at[source(px, pipes, j)].set(mine[j])
    every = lax.all_gather(whole, "pipe")
    whole = every[0]
    for p in range(1, pipes):
        whole = jax.vmap(merge)(whole, every[p])
    total = whole
    for k in range(1, tensors):
        total = jax.vmap(merge)(total, tensor_permute(whole, k))
    row_loss = (jnp.log(total[:, 1]) + total[:, 0] - total[:, 2]).reshape(-1)
    dlogits = []
    for j in range(pipes):
        m, s, _ = total[source(px, pipes, j)]
        hit = (columns == local_targets[j][:, None]).astype(F32)
        scaled = jnp.exp(logits[j] - m[:, None]) / s[:, None] - hit
        dlogits.append((local_scale[j][:, None] * scaled).astype(BF16))
    sums = [None] * tensors
    for k in range(tensors - 1, -1, -1):
        acc = 0
        for j in range(pipes - 1, -1, -1):
            part = lax.dot_general(dlogits[j], w_out[k], ROWS_BY_ROWS, preferred_element_type=F32)
            if j:
                part = lax.ppermute(part.astype(BF16), "pipe", [(b, a) for a, b in partners(pipes, j)]).astype(F32)
            acc += part
        if k:
            acc = tensor_permute(acc.astype(BF16), k).astype(F32)
        sums[k] = acc
    return sum(sums[1:], sums[0]).astype(BF16), row_loss


def block(ref, place, k, width):
    return ref[pl.ds(pl.multiple_of(place[k] * width, width), width), :]


def columns_of(row_list):
    rows = row_list[0].shape[1]
    table = jnp.concatenate(row_list + [jnp.zeros((128 - len(row_list), rows), F32)], axis=0)
    table = jnp.transpose(table)
    return [table[:, i : i + 1] for i in range(len(row_list))]


def rows_of(columns):
    lane = lax.broadcasted_iota(jnp.int32, (columns[0].shape[0], 128), 1)
    wide = jnp.zeros(lane.shape, F32)
    for i, column in enumerate(columns):
        wide = jnp.where(lane == i, column, wide)
    return jnp.transpose(wide)[:8, :]


def hits(targets, shape):
    return lax.broadcasted_iota(jnp.int32, shape, 1) == targets[:, :1]


def fetch_kernel(place, weight, targets, scale, kept, mine, other, weights_of, mine_rows, other0, other1, other2, sent, sems):
    rows, width = other0.shape
    other_rows = (other0, other1, other2)
    copies = []
    for k in (3, 2, 1, 0):
        part = pl.ds(pl.multiple_of(place[k] * width, width), width)
        copies.append((k, pltpu.make_async_copy(weight.at[part], kept.at[part], sems.at[k])))
        copies[-1][1].start()
    lower = place[5] == 0
    halves = [(targets[:, :rows] - place[4]).astype(F32), (targets[:, rows:] - place[4]).astype(F32)]
    own = jnp.where(lower, halves[0], halves[1])
    theirs = jnp.where(lower, halves[1], halves[0])
    own, theirs = [column.astype(jnp.int32) for column in columns_of([own, theirs])]
    mine[...] = jnp.broadcast_to(own, mine.shape)
    other[...] = jnp.broadcast_to(theirs, other.shape)
    weights_of[...] = jnp.where(lower, scale[:, :rows], scale[:, rows:])
    entry = lax.broadcasted_iota(jnp.int32, (2 * rows, kept.shape[1]), 1)
    one_hot = (entry == jnp.concatenate([theirs, own], axis=0)).astype(F32).astype(BF16)
    for k, copy in copies:
        copy.wait()
        both = lax.dot_general(one_hot, block(kept, place, k, width), ROWS_BY_ROWS, preferred_element_type=F32)
        both = both.astype(BF16)
        if k == 3:
            sent[...] = both
        else:
            other_rows[k][...] = both[:rows]
            mine_rows[k] = both[rows:]


def stack_kernel(a, b, out):
    rows = a.shape[0]
    out[:rows] = a[...]
    out[rows:] = b[...]


def add_kernel(*refs):
    *ins, out = refs
    out[...] = sum((a[: out.shape[0]] for a in ins[1:]), ins[0][: out.shape[0]])


def softmax_part(acc, targets):
    hit = hits(targets, acc.shape)
    top = jnp.max(acc, axis=1, keepdims=True)
    shifted = jnp.exp(acc - top)
    total = jnp.sum(shifted, axis=1, keepdims=True)
    label = jnp.sum(jnp.where(hit, acc, 0.0), axis=1, keepdims=True)
    return rows_of([top, total, label]), jnp.where(hit, 0.0, shifted).astype(BF16)


def own_kernel(place, kept, targets, a, b, c, d, stats, sums):
    acc = 0
    for k, shard in enumerate((a, b, c, d)):
        acc += jnp.dot(shard[...], block(kept, place, k, shard.shape[1]), preferred_element_type=F32)
    stats[...], others = softmax_part(acc, targets)
    for k in range(sums.shape[0]):
        weights = block(kept, place, k, sums.shape[2])
        sums[k] = lax.dot_general(others, weights, ROWS_BY_ROWS, preferred_element_type=F32)


def start_kernel(place, kept, a, bc, out):
    rows, width = a.shape
    acc = jnp.dot(a[...], block(kept, place, 0, width), preferred_element_type=F32)
    acc += jnp.dot(bc[:rows], block(kept, place, 1, width), preferred_element_type=F32)
    acc += jnp.dot(bc[rows:], block(kept, place, 2, width), preferred_element_type=F32)
    out[...] = acc


def peer_kernel(place, kept, targets, partial, d, block0, block21, block3):
    rows, width = d.shape
    acc = partial[...] + jnp.dot(d[...], block(kept, place, 3, width), preferred_element_type=F32)
    stats, others = softmax_part(acc, targets)
    block3[rows:] = with_tail(stats, width)
    for k, out in ((3, block3.at[:rows]), (2, block21.at[:rows]), (1, block21.at[rows:]), (0, block0)):
        weights = block(kept, place, k, width)
        out[...] = lax.dot_general(others, weights, ROWS_BY_ROWS, preferred_element_type=F32).astype(BF16)


def join(a, b):
    top = jnp.maximum(a[0], b[0])
    return top, a[1] * jnp.exp(a[0] - top) + b[1] * jnp.exp(b[0] - top), a[2] + b[2]


def as_rows(a):
    return a[0:1], a[1:2], a[2:3]


def with_tail(stats, width):
    high = stats.astype(BF16)
    rest = stats - high.astype(F32)
    middle = rest.astype(BF16)
    low = (rest - middle.astype(F32)).astype(BF16)
    pad = jnp.zeros((8, width - stats.shape[1]), F32)
    terms = [jnp.concatenate([term.astype(F32), pad], axis=1) for term in (high, middle, low)]
    return jnp.concatenate(terms + [jnp.zeros_like(terms[0])], axis=0).astype(BF16)


def from_tail(ref, rows):
    tail = ref[rows:].astype(F32)[:, :rows]
    return tail[0:8] + tail[8:16] + tail[16:24]


def pair_kernel(own_stats, got, sums, pair, sent):
    rows = own_stats.shape[1]
    theirs = from_tail(got, rows)
    mine, theirs = as_rows(own_stats[...]), as_rows(theirs)
    both = join(mine, theirs)
    stats = jnp.concatenate(list(both) + [mine[0], theirs[0]] + [jnp.zeros((3, rows), F32)], axis=0)
    pair[...] = stats
    sent[rows:] = with_tail(stats, sent.shape[1])
    near, far = columns_of([jnp.exp(mine[0] - both[0]), jnp.exp(theirs[0] - both[0])])
    sent[:rows] = (near * sums[3] + far * got[:rows].astype(F32)).astype(BF16)


def join_kernel(pair, got, out):
    rows = pair.shape[1]
    near = as_rows(from_tail(got, rows))
    both = join(as_rows(pair[...]), near)
    out[...] = jnp.concatenate(list(both) + [near[0], jnp.zeros((4, rows), F32)], axis=0)


def block_sum(by, sums, got, picked, k):
    return by[0] * sums[k] + by[1] * got[...].astype(F32) + by[3] * picked[k].astype(F32)


def scale_kernel(scale, pair, half, far, sums, got, relayed, picked, near_picked, loss, columns, second, first):
    rows = first.shape[0]
    top, total, label = join(as_rows(half[...]), as_rows(far[...]))
    loss[...] = jnp.log(total) + top - label
    weighted = scale[...] / total
    factors = [weighted * jnp.exp(a - top) for a in (pair[3:4], pair[4:5], half[3:4])]
    missing = scale[...] * (jnp.exp(label - top) / total - 1.0)
    by = columns_of(factors + [missing])
    for i, column in enumerate(by):
        columns[i] = jnp.broadcast_to(column, columns.shape[1:])
    here = block_sum(by, sums, got.at[:rows], picked, 2)
    here += by[2] * relayed[:rows].astype(F32) + by[3] * near_picked[rows:].astype(F32)
    second[...] = here.astype(BF16)
    first[...] = block_sum(by, sums, got.at[rows:], picked, 1).astype(BF16)


def last_kernel(place, columns, sums, got, picked, theirs, first, second, loss, other_loss, out, row_loss):
    by = [columns[i][:, :1] for i in range(4)]
    here = block_sum(by, sums, got, picked, 0) + by[3] * theirs[...].astype(F32)
    out[...] = (here + first[...].astype(F32) + second[...].astype(F32)).astype(BF16)
    lower = place[5] == 0
    row_loss[: out.shape[0]] = jnp.where(lower, loss[...], other_loss[...])[0]
    row_loss[out.shape[0] :] = jnp.where(lower, other_loss[...], loss[...])[0]


def two_by_four(hidden, weight, targets, row_weight):
    tensors = lax.axis_size("tensor")
    px, tz = lax.axis_index("pipe"), lax.axis_index("tensor")
    rows, width = hidden.shape
    vocab_dev = weight.shape[1]

    def along(a, k):
        return lax.ppermute(a, "tensor", partners(tensors, k))

    def across(a):
        return lax.ppermute(a, "pipe", [(0, 1), (1, 0)])

    def after(a, b):
        return lax.optimization_barrier((a, b))[0]

    def call(kernel, outs, ins, *args, scratch=()):
        return pl.pallas_call(
            kernel,
            out_shape=outs,
            in_specs=ins,
            out_specs=jax.tree.map(lambda _: VMEM, outs),
            scratch_shapes=list(scratch),
            compiler_params=LIMIT,
        )(*args)

    def shape(*dims, dtype=F32):
        return jax.ShapeDtypeStruct(dims, dtype)

    place = [tz ^ k for k in range(tensors)] + [(px * tensors + tz) * vocab_dev, px]
    place = jnp.stack(place).astype(jnp.int32)
    piece = shape(rows, width, dtype=BF16)
    two = shape(2 * rows, width, dtype=BF16)
    tailed = shape(rows + 32, width, dtype=BF16)
    wide = shape(rows, 128, dtype=jnp.int32)

    z2 = along(hidden, 2)
    z1 = along(hidden, 1)
    x0 = across(hidden)
    kept, mine, other, scale, mine_rows, *other_rows, sent_rows = call(
        fetch_kernel,
        [pltpu.VMEM(weight.shape, BF16), wide, wide, shape(1, rows),
         shape(3, rows, width, dtype=BF16), piece, piece, piece, two],
        [SMEM, HBM, VMEM, VMEM],
        place, pltpu.with_memory_space_constraint(weight, pltpu.HBM), targets.reshape(1, -1), row_weight.reshape(1, -1),
        scratch=[pltpu.SemaphoreType.DMA((4,))],
    )
    z2 = after(z2, scale)
    z3 = along(z2, 1)
    x12 = across(call(stack_kernel, two, [VMEM] * 2, after(z1, x0), z2))
    x3 = across(z3)

    relayed_rows = along(after(sent_rows, z3), 1)

    own_stats, sums = call(
        own_kernel, [shape(8, rows), shape(tensors, rows, width)], [SMEM] + [VMEM] * 6,
        place, kept, mine, hidden, z1, z2, z3,
    )
    partial = call(start_kernel, shape(rows, vocab_dev), [SMEM] + [VMEM] * 3, place, kept, x0, x12)
    other = after(other, (own_stats, relayed_rows))
    block0, block21, block3 = call(
        peer_kernel, [piece, two, tailed], [SMEM] + [VMEM] * 4, place, kept, other, partial, x3
    )

    far_rows = along(call(add_kernel, piece, [VMEM] * 2, other_rows[2], relayed_rows), 2)
    near_rows = along(after(other_rows[1], partial), 1)
    got3 = across(block3)
    got21 = across(after(block21, got3))
    pair, relayed = call(pair_kernel, [shape(8, rows), tailed], [VMEM] * 3, after(own_stats, near_rows), got3, sums)
    relayed = along(relayed, 1)
    half = call(join_kernel, shape(8, rows), [VMEM] * 2, pair, relayed)
    far = along(half, 2)
    loss, columns, second, first = call(
        scale_kernel,
        [shape(1, rows), shape(4, rows, 128), piece, piece],
        [VMEM] * 9,
        scale, pair, half, after(far, far_rows), sums, got21, relayed, mine_rows, relayed_rows,
    )
    second = along(second, 2)
    got0 = across(block0)
    first = along(after(first, got0), 1)
    picked = call(add_kernel, piece, [VMEM] * 3, other_rows[0], near_rows, far_rows)
    picked = across(after(picked, got0))
    other_loss = across(after(loss, first))
    grad, row_loss = call(
        last_kernel, [piece, shape(2 * rows)], [SMEM] + [VMEM] * 9,
        place, columns, sums, got0, mine_rows, picked, first, second, loss, other_loss,
    )
    return grad, row_loss


def per_device(hidden, weight, targets, row_weight):
    if lax.axis_size("pipe") == 2 and lax.axis_size("tensor") == 4:
        return two_by_four(hidden, weight, targets, row_weight)
    return any_mesh(hidden, weight, targets, row_weight)


def solution(mesh):
    in_specs = (P(("dp", "pipe"), "tensor"), P(None, ("pipe", "tensor")), P("dp"), P("dp"))
    out_specs = (P(("dp", "pipe"), "tensor"), P("dp"))
    return jax.shard_map(
        per_device, mesh=mesh, in_specs=in_specs, out_specs=out_specs, check_vma=False
    )
```

```python
import jax
import jax.numpy as jnp
from jax import lax
from jax.experimental import pallas as pl
from jax.experimental.pallas import tpu as pltpu
from jax.sharding import PartitionSpec as P

BF16, F32 = jnp.bfloat16, jnp.float32
ROWS_BY_ROWS = (((1,), (1,)), ((), ()))
VMEM = pl.BlockSpec(memory_space=pltpu.VMEM)
SMEM = pl.BlockSpec(memory_space=pltpu.SMEM)
HBM = pl.BlockSpec(memory_space=pltpu.HBM)
LIMIT = pltpu.CompilerParams(vmem_limit_bytes=24 * 2**20)


def partners(n, k):
    if n & (n - 1):
        return [(i, (i + k) % n) for i in range(n)]
    return [(i, i ^ k) for i in range(n)]


def source(me, n, k):
    if n & (n - 1):
        return lax.rem(me - k + n, n)
    return me ^ k


def target(me, n, k):
    if n & (n - 1):
        return lax.rem(me + k, n)
    return me ^ k


def merge(a, b):
    top = jnp.maximum(a[0], b[0])
    total = a[1] * jnp.exp(a[0] - top) + b[1] * jnp.exp(b[0] - top)
    return jnp.stack([top, total, a[2] + b[2]])


def any_mesh(hidden, weight, targets, row_weight):
    pipes, tensors = lax.axis_size("pipe"), lax.axis_size("tensor")
    px, tz = lax.axis_index("pipe"), lax.axis_index("tensor")
    rows, width = hidden.shape
    vocab_dev = weight.shape[1]
    offset = (px * tensors + tz) * vocab_dev

    w_in = [lax.dynamic_slice_in_dim(weight, source(tz, tensors, k) * width, width, 0) for k in range(tensors)]
    w_out = [lax.dynamic_slice_in_dim(weight, target(tz, tensors, k) * width, width, 0) for k in range(tensors)]

    def tensor_permute(a, k):
        return a if k == 0 else lax.ppermute(a, "tensor", partners(tensors, k))

    def pipe_permute(a, j):
        return a if j == 0 else lax.ppermute(a, "pipe", partners(pipes, j))

    local_targets = [targets.reshape(pipes, rows)[source(px, pipes, j)] for j in range(pipes)]
    local_scale = [row_weight.reshape(pipes, rows)[source(px, pipes, j)] for j in range(pipes)]
    columns = lax.broadcasted_iota(jnp.int32, (rows, vocab_dev), 1) + offset
    arrived = [tensor_permute(hidden, k) for k in range(tensors)]
    logits, stats = [], []
    for j in range(pipes):
        acc = 0
        for k in range(tensors):
            acc += jnp.dot(pipe_permute(arrived[k], j), w_in[k], preferred_element_type=F32)
        logits.append(acc)
        m = jnp.max(acc, axis=1)
        s = jnp.sum(jnp.exp(acc - m[:, None]), axis=1)
        label = jnp.sum(jnp.where(columns == local_targets[j][:, None], acc, 0.0), axis=1)
        stats.append(jnp.stack([m, s, label]))
    mine = jnp.stack(stats)
    whole = jnp.zeros_like(mine)
    for j in range(pipes):
        whole = whole.at[source(px, pipes, j)].set(mine[j])
    every = lax.all_gather(whole, "pipe")
    whole = every[0]
    for p in range(1, pipes):
        whole = jax.vmap(merge)(whole, every[p])
    total = whole
    for k in range(1, tensors):
        total = jax.vmap(merge)(total, tensor_permute(whole, k))
    row_loss = (jnp.log(total[:, 1]) + total[:, 0] - total[:, 2]).reshape(-1)
    dlogits = []
    for j in range(pipes):
        m, s, _ = total[source(px, pipes, j)]
        hit = (columns == local_targets[j][:, None]).astype(F32)
        scaled = jnp.exp(logits[j] - m[:, None]) / s[:, None] - hit
        dlogits.append((local_scale[j][:, None] * scaled).astype(BF16))
    sums = [None] * tensors
    for k in range(tensors - 1, -1, -1):
        acc = 0
        for j in range(pipes - 1, -1, -1):
            part = lax.dot_general(dlogits[j], w_out[k], ROWS_BY_ROWS, preferred_element_type=F32)
            if j:
                part = lax.ppermute(part.astype(BF16), "pipe", [(b, a) for a, b in partners(pipes, j)]).astype(F32)
            acc += part
        if k:
            acc = tensor_permute(acc.astype(BF16), k).astype(F32)
        sums[k] = acc
    return sum(sums[1:], sums[0]).astype(BF16), row_loss


def block(ref, place, k, width):
    return ref[pl.ds(pl.multiple_of(place[k] * width, width), width), :]


def columns_of(row_list):
    rows = row_list[0].shape[1]
    table = jnp.concatenate(row_list + [jnp.zeros((128 - len(row_list), rows), F32)], axis=0)
    table = jnp.transpose(table)
    return [table[:, i : i + 1] for i in range(len(row_list))]


def rows_of(columns):
    lane = lax.broadcasted_iota(jnp.int32, (columns[0].shape[0], 128), 1)
    wide = jnp.zeros(lane.shape, F32)
    for i, column in enumerate(columns):
        wide = jnp.where(lane == i, column, wide)
    return jnp.transpose(wide)[:8, :]


def hits(targets, shape):
    return lax.broadcasted_iota(jnp.int32, shape, 1) == targets[:, :1]


def fetch_kernel(place, weight, kept, sem):
    @pl.when(place[6] == 0)
    def _():
        copy = pltpu.make_async_copy(weight, kept, sem)
        copy.start()
        copy.wait()


def targets_kernel(place, weight, targets, scale, fetched, kept, mine, other, weights_of, sem):
    copy = pltpu.make_async_copy(weight, kept, sem)

    @pl.when(place[6] == 1)
    def _():
        copy.start()

    rows = mine.shape[0]
    lower = place[5] == 0
    targets, scale = targets[...].reshape(1, -1), scale[...].reshape(1, -1)
    halves = [(targets[:, :rows] - place[4]).astype(F32), (targets[:, rows:] - place[4]).astype(F32)]
    own = jnp.where(lower, halves[0], halves[1])
    theirs = jnp.where(lower, halves[1], halves[0])
    own, theirs = [column.astype(jnp.int32) for column in columns_of([own, theirs])]
    mine[...] = jnp.broadcast_to(own, mine.shape)
    other[...] = jnp.broadcast_to(theirs, other.shape)
    weights_of[...] = jnp.where(lower, scale[:, :rows], scale[:, rows:])

    @pl.when(place[6] == 1)
    def _():
        copy.wait()


def pick_kernel(place, kept, mine, other, mine_rows, other0, other1, other2, sent):
    rows, width = other0.shape
    other_rows = (other0, other1, other2)
    column = jnp.concatenate([other[:, :1], mine[:, :1]], axis=0)
    entry = lax.broadcasted_iota(jnp.int32, (2 * rows, kept.shape[1]), 1)
    one_hot = (entry == column).astype(F32).astype(BF16)
    for k in (3, 2, 1, 0):
        both = lax.dot_general(one_hot, block(kept, place, k, width), ROWS_BY_ROWS, preferred_element_type=F32)
        both = both.astype(BF16)
        if k == 3:
            sent[...] = both
        else:
            other_rows[k][...] = both[:rows]
            mine_rows[k] = both[rows:]


def stack_kernel(a, b, out):
    rows = a.shape[0]
    out[:rows] = a[...]
    out[rows:] = b[...]


def add_kernel(a, b, out):
    rows = a.shape[0]
    out[:rows] = a[...] + b[:rows]
    out[rows:] = jnp.zeros((out.shape[0] - rows, out.shape[1]), BF16)


def last_rows_kernel(a, b, c, out):
    out[...] = a[...] + b[...] + c[: out.shape[0]]


def softmax_part(acc, targets):
    hit = hits(targets, acc.shape)
    top = jnp.max(acc, axis=1, keepdims=True)
    shifted = jnp.exp(acc - top)
    total = jnp.sum(shifted, axis=1, keepdims=True)
    label = jnp.sum(jnp.where(hit, acc, 0.0), axis=1, keepdims=True)
    return rows_of([top, total, label]), jnp.where(hit, 0.0, shifted).astype(BF16)


def own_kernel(place, kept, targets, a, b, c, d, stats, sums):
    acc = 0
    for k, shard in enumerate((a, b, c, d)):
        acc += jnp.dot(shard[...], block(kept, place, k, shard.shape[1]), preferred_element_type=F32)
    stats[...], others = softmax_part(acc, targets)
    for k in range(sums.shape[0]):
        weights = block(kept, place, k, sums.shape[2])
        sums[k] = lax.dot_general(others, weights, ROWS_BY_ROWS, preferred_element_type=F32)


def start_kernel(place, kept, a, bc, out):
    rows, width = a.shape
    acc = jnp.dot(a[...], block(kept, place, 0, width), preferred_element_type=F32)
    acc += jnp.dot(bc[:rows], block(kept, place, 1, width), preferred_element_type=F32)
    acc += jnp.dot(bc[rows:], block(kept, place, 2, width), preferred_element_type=F32)
    out[...] = acc


def peer_kernel(place, kept, targets, partial, d, block0, block21, block3):
    rows, width = d.shape
    acc = partial[...] + jnp.dot(d[...], block(kept, place, 3, width), preferred_element_type=F32)
    stats, others = softmax_part(acc, targets)
    block3[rows:] = with_tail(as_rows(stats), width)
    for k, out in ((3, block3.at[:rows]), (2, block21.at[:rows]), (1, block21.at[rows:]), (0, block0)):
        weights = block(kept, place, k, width)
        out[...] = lax.dot_general(others, weights, ROWS_BY_ROWS, preferred_element_type=F32).astype(BF16)


def join(a, b):
    top = jnp.maximum(a[0], b[0])
    return top, a[1] * jnp.exp(a[0] - top) + b[1] * jnp.exp(b[0] - top), a[2] + b[2]


def as_rows(a):
    return a[0:1], a[1:2], a[2:3]


def with_tail(stats, width):
    high = [row.astype(BF16).astype(F32) for row in stats]
    rest = [row - term for row, term in zip(stats, high)]
    middle = [row.astype(BF16).astype(F32) for row in rest]
    low = [row - term for row, term in zip(rest, middle)]
    rows = jnp.concatenate(high + middle + low + [jnp.zeros((7, stats[0].shape[1]), F32)], axis=0)
    return jnp.concatenate([rows, jnp.zeros((16, width - rows.shape[1]), F32)], axis=1).astype(BF16)


def from_tail(ref, rows):
    tail = ref[rows:].astype(F32)[:, :rows]
    return [tail[i : i + 1] + tail[i + 3 : i + 4] + tail[i + 6 : i + 7] for i in range(3)]


def pair_kernel(own_stats, got, sums, pair, sent):
    rows = own_stats.shape[1]
    theirs = from_tail(got, rows)
    mine = as_rows(own_stats[...])
    both = join(mine, theirs)
    stats = jnp.concatenate(list(both) + [mine[0], theirs[0]] + [jnp.zeros((3, rows), F32)], axis=0)
    pair[...] = stats
    sent[rows:] = with_tail(both, sent.shape[1])
    near, far = columns_of([jnp.exp(mine[0] - both[0]), jnp.exp(theirs[0] - both[0])])
    sent[:rows] = (near * sums[3] + far * got[:rows].astype(F32)).astype(BF16)


def join_kernel(pair, got, out):
    rows = pair.shape[1]
    near = from_tail(got, rows)
    both = join(as_rows(pair[...]), near)
    out[...] = jnp.concatenate(list(both) + [near[0], jnp.zeros((4, rows), F32)], axis=0)


def block_sum(by, sums, got, picked, k):
    return by[0] * sums[k] + by[1] * got[...].astype(F32) + by[3] * picked[k].astype(F32)


def scale_kernel(scale, pair, half, far, sums, got, relayed, picked, near_picked, loss, columns, second, first):
    rows = first.shape[0]
    top, total, label = join(as_rows(half[...]), as_rows(far[...]))
    loss[...] = jnp.log(total) + top - label
    weighted = scale[...] / total
    factors = [weighted * jnp.exp(a - top) for a in (pair[3:4], pair[4:5], half[3:4])]
    missing = scale[...] * (jnp.exp(label - top) / total - 1.0)
    by = columns_of(factors + [missing])
    for i, column in enumerate(by):
        columns[i] = jnp.broadcast_to(column, columns.shape[1:])
    here = block_sum(by, sums, got.at[:rows], picked, 2)
    here += by[2] * relayed[:rows].astype(F32) + by[3] * near_picked[rows:].astype(F32)
    second[...] = here.astype(BF16)
    first[...] = block_sum(by, sums, got.at[rows:], picked, 1).astype(BF16)


def second_kernel(columns, sums, got, picked, second, out):
    by = [columns[i][:, :1] for i in range(4)]
    out[...] = block_sum(by, sums, got, picked, 0) + second[...].astype(F32)


def last_kernel(place, columns, partial, first, theirs, loss, other_loss, out, row_loss):
    here = partial[...] + first[...].astype(F32) + columns[3][:, :1] * theirs[...].astype(F32)
    out[...] = here.astype(BF16)
    lower = place[5] == 0
    row_loss[: out.shape[0]] = jnp.where(lower, loss[...], other_loss[...])[0]
    row_loss[out.shape[0] :] = jnp.where(lower, other_loss[...], loss[...])[0]


def two_by_four(hidden, weight, targets, row_weight):
    tensors = lax.axis_size("tensor")
    px, tz = lax.axis_index("pipe"), lax.axis_index("tensor")
    rows, width = hidden.shape
    vocab_dev = weight.shape[1]

    def along(a, k):
        return lax.ppermute(a, "tensor", partners(tensors, k))

    def across(a):
        return lax.ppermute(a, "pipe", [(0, 1), (1, 0)])

    def after(a, b):
        return lax.optimization_barrier((a, b))[0]

    def call(kernel, outs, ins, *args, scratch=(), aliases=None):
        return pl.pallas_call(
            kernel,
            out_shape=outs,
            in_specs=ins,
            out_specs=jax.tree.map(lambda _: VMEM, outs),
            scratch_shapes=list(scratch),
            input_output_aliases=aliases or {},
            compiler_params=LIMIT,
        )(*args)

    def shape(*dims, dtype=F32):
        return jax.ShapeDtypeStruct(dims, dtype)

    place = [tz ^ k for k in range(tensors)] + [(px * tensors + tz) * vocab_dev, px, lax.axis_index("dp") % 2]
    place = jnp.stack(place).astype(jnp.int32)
    piece = shape(rows, width, dtype=BF16)
    two = shape(2 * rows, width, dtype=BF16)
    tailed = shape(rows + 16, width, dtype=BF16)
    wide = shape(rows, 128, dtype=jnp.int32)

    weight = pltpu.with_memory_space_constraint(weight, pltpu.HBM)
    dma = [pltpu.SemaphoreType.DMA]
    kept = call(fetch_kernel, pltpu.VMEM(weight.shape, BF16), [SMEM, HBM], place, weight, scratch=dma)
    hidden = after(hidden, kept)
    z2 = along(hidden, 2)
    z1 = along(hidden, 1)
    x0 = across(hidden)
    kept, mine, other, scale = call(
        targets_kernel,
        [pltpu.VMEM(weight.shape, BF16), wide, wide, shape(1, rows)],
        [SMEM, HBM, VMEM, VMEM, VMEM],
        place, weight, targets, row_weight, kept, scratch=dma, aliases={4: 0},
    )
    z2 = after(z2, scale)
    z3 = along(z2, 1)
    x12 = across(call(stack_kernel, two, [VMEM] * 2, after(z1, x0), z2))
    mine_rows, *other_rows, sent_rows = call(
        pick_kernel, [shape(3, rows, width, dtype=BF16), piece, piece, piece, two], [SMEM] + [VMEM] * 3,
        after(place, z2), kept, mine, other,
    )
    x3 = across(after(z3, sent_rows))

    relayed_rows = along(after(sent_rows, z3), 1)

    own_stats, sums = call(
        own_kernel, [shape(8, rows), shape(tensors, rows, width)], [SMEM] + [VMEM] * 6,
        place, kept, mine, hidden, z1, z2, z3,
    )
    partial = call(start_kernel, shape(rows, vocab_dev), [SMEM] + [VMEM] * 3, place, kept, x0, x12)
    other = after(other, (own_stats, relayed_rows))
    block0, block21, block3 = call(
        peer_kernel, [piece, two, tailed], [SMEM] + [VMEM] * 4, place, kept, other, partial, x3
    )
    far_rows = along(call(add_kernel, shape(rows + 32, width, dtype=BF16), [VMEM] * 2, other_rows[2], relayed_rows), 2)
    got3 = across(block3)
    pair, relayed = call(pair_kernel, [shape(8, rows), tailed], [VMEM] * 3, own_stats, got3, sums)
    relayed = along(relayed, 1)
    got21 = across(after(block21, pair))
    half = call(join_kernel, shape(8, rows), [VMEM] * 2, pair, after(relayed, far_rows))
    far = along(half, 2)
    near_rows = along(after(other_rows[1], half), 1)
    loss, columns, second, first = call(
        scale_kernel,
        [shape(1, rows), shape(4, rows, 128), piece, piece],
        [VMEM] * 9,
        scale, pair, half, far, sums, got21, relayed, mine_rows, relayed_rows,
    )
    second = along(second, 2)
    got0 = across(block0)
    picked = across(call(last_rows_kernel, piece, [VMEM] * 3, other_rows[0], near_rows, far_rows))
    first = along(first, 1)
    other_loss = across(loss)
    partial = call(second_kernel, shape(rows, width), [VMEM] * 5, columns, sums, got0, mine_rows, second)
    grad, row_loss = call(
        last_kernel, [piece, shape(2 * rows)], [SMEM] + [VMEM] * 6,
        place, columns, partial, first, picked, loss, other_loss,
    )
    return grad, row_loss


def per_device(hidden, weight, targets, row_weight):
    if lax.axis_size("pipe") == 2 and lax.axis_size("tensor") == 4:
        return two_by_four(hidden, weight, targets, row_weight)
    return any_mesh(hidden, weight, targets, row_weight)


def solution(mesh):
    in_specs = (P(("dp", "pipe"), "tensor"), P(None, ("pipe", "tensor")), P("dp"), P("dp"))
    out_specs = (P(("dp", "pipe"), "tensor"), P("dp"))
    return jax.shard_map(
        per_device, mesh=mesh, in_specs=in_specs, out_specs=out_specs, check_vma=False
    )
```

```python
import jax
import jax.numpy as jnp
from jax import lax
from jax.experimental import pallas as pl
from jax.experimental.pallas import tpu as pltpu
from jax.sharding import PartitionSpec as P

BF16, F32 = jnp.bfloat16, jnp.float32
ROWS_BY_ROWS = (((1,), (1,)), ((), ()))
VMEM = pl.BlockSpec(memory_space=pltpu.VMEM)
SMEM = pl.BlockSpec(memory_space=pltpu.SMEM)
HBM = pl.BlockSpec(memory_space=pltpu.HBM)
LIMIT = pltpu.CompilerParams(vmem_limit_bytes=24 * 2**20)


def partners(n, k):
    if n & (n - 1):
        return [(i, (i + k) % n) for i in range(n)]
    return [(i, i ^ k) for i in range(n)]


def source(me, n, k):
    if n & (n - 1):
        return lax.rem(me - k + n, n)
    return me ^ k


def target(me, n, k):
    if n & (n - 1):
        return lax.rem(me + k, n)
    return me ^ k


def merge(a, b):
    top = jnp.maximum(a[0], b[0])
    total = a[1] * jnp.exp(a[0] - top) + b[1] * jnp.exp(b[0] - top)
    return jnp.stack([top, total, a[2] + b[2]])


def any_mesh(hidden, weight, targets, row_weight):
    pipes, tensors = lax.axis_size("pipe"), lax.axis_size("tensor")
    px, tz = lax.axis_index("pipe"), lax.axis_index("tensor")
    rows, width = hidden.shape
    vocab_dev = weight.shape[1]
    offset = (px * tensors + tz) * vocab_dev

    w_in = [lax.dynamic_slice_in_dim(weight, source(tz, tensors, k) * width, width, 0) for k in range(tensors)]
    w_out = [lax.dynamic_slice_in_dim(weight, target(tz, tensors, k) * width, width, 0) for k in range(tensors)]

    def tensor_permute(a, k):
        return a if k == 0 else lax.ppermute(a, "tensor", partners(tensors, k))

    def pipe_permute(a, j):
        return a if j == 0 else lax.ppermute(a, "pipe", partners(pipes, j))

    local_targets = [targets.reshape(pipes, rows)[source(px, pipes, j)] for j in range(pipes)]
    local_scale = [row_weight.reshape(pipes, rows)[source(px, pipes, j)] for j in range(pipes)]
    columns = lax.broadcasted_iota(jnp.int32, (rows, vocab_dev), 1) + offset
    arrived = [tensor_permute(hidden, k) for k in range(tensors)]
    logits, stats = [], []
    for j in range(pipes):
        acc = 0
        for k in range(tensors):
            acc += jnp.dot(pipe_permute(arrived[k], j), w_in[k], preferred_element_type=F32)
        logits.append(acc)
        m = jnp.max(acc, axis=1)
        s = jnp.sum(jnp.exp(acc - m[:, None]), axis=1)
        label = jnp.sum(jnp.where(columns == local_targets[j][:, None], acc, 0.0), axis=1)
        stats.append(jnp.stack([m, s, label]))
    mine = jnp.stack(stats)
    whole = jnp.zeros_like(mine)
    for j in range(pipes):
        whole = whole.at[source(px, pipes, j)].set(mine[j])
    every = lax.all_gather(whole, "pipe")
    whole = every[0]
    for p in range(1, pipes):
        whole = jax.vmap(merge)(whole, every[p])
    total = whole
    for k in range(1, tensors):
        total = jax.vmap(merge)(total, tensor_permute(whole, k))
    row_loss = (jnp.log(total[:, 1]) + total[:, 0] - total[:, 2]).reshape(-1)
    dlogits = []
    for j in range(pipes):
        m, s, _ = total[source(px, pipes, j)]
        hit = (columns == local_targets[j][:, None]).astype(F32)
        scaled = jnp.exp(logits[j] - m[:, None]) / s[:, None] - hit
        dlogits.append((local_scale[j][:, None] * scaled).astype(BF16))
    sums = [None] * tensors
    for k in range(tensors - 1, -1, -1):
        acc = 0
        for j in range(pipes - 1, -1, -1):
            part = lax.dot_general(dlogits[j], w_out[k], ROWS_BY_ROWS, preferred_element_type=F32)
            if j:
                part = lax.ppermute(part.astype(BF16), "pipe", [(b, a) for a, b in partners(pipes, j)]).astype(F32)
            acc += part
        if k:
            acc = tensor_permute(acc.astype(BF16), k).astype(F32)
        sums[k] = acc
    return sum(sums[1:], sums[0]).astype(BF16), row_loss


def block(ref, place, k, width):
    return ref[pl.ds(pl.multiple_of(place[k] * width, width), width), :]


def columns_of(row_list):
    rows = row_list[0].shape[1]
    table = jnp.concatenate(row_list + [jnp.zeros((128 - len(row_list), rows), F32)], axis=0)
    table = jnp.transpose(table)
    return [table[:, i : i + 1] for i in range(len(row_list))]


def rows_of(columns):
    lane = lax.broadcasted_iota(jnp.int32, (columns[0].shape[0], 128), 1)
    wide = jnp.zeros(lane.shape, F32)
    for i, column in enumerate(columns):
        wide = jnp.where(lane == i, column, wide)
    return jnp.transpose(wide)[:8, :]


def hits(targets, shape):
    return lax.broadcasted_iota(jnp.int32, shape, 1) == targets[:, :1]


def fetch_kernel(place, weight, kept, sem):
    @pl.when(place[6] == 0)
    def _():
        copy = pltpu.make_async_copy(weight, kept, sem)
        copy.start()
        copy.wait()


def targets_kernel(place, weight, targets, scale, fetched, kept, mine, other, weights_of, sem):
    copy = pltpu.make_async_copy(weight, kept, sem)

    @pl.when(place[6] == 1)
    def _():
        copy.start()

    rows = mine.shape[0]
    lower = place[5] == 0
    targets, scale = targets[...].reshape(1, -1), scale[...].reshape(1, -1)
    halves = [(targets[:, :rows] - place[4]).astype(F32), (targets[:, rows:] - place[4]).astype(F32)]
    own = jnp.where(lower, halves[0], halves[1])
    theirs = jnp.where(lower, halves[1], halves[0])
    own, theirs = [column.astype(jnp.int32) for column in columns_of([own, theirs])]
    mine[...] = jnp.broadcast_to(own, mine.shape)
    other[...] = jnp.broadcast_to(theirs, other.shape)
    weights_of[...] = jnp.where(lower, scale[:, :rows], scale[:, rows:])

    @pl.when(place[6] == 1)
    def _():
        copy.wait()


def pick_kernel(place, kept, mine, other, mine_rows, other0, other1, other2, sent):
    rows, width = other0.shape
    other_rows = (other0, other1, other2)
    column = jnp.concatenate([other[:, :1], mine[:, :1]], axis=0)
    entry = lax.broadcasted_iota(jnp.int32, (2 * rows, kept.shape[1]), 1)
    one_hot = (entry == column).astype(F32).astype(BF16)
    for k in (3, 2, 1, 0):
        both = lax.dot_general(one_hot, block(kept, place, k, width), ROWS_BY_ROWS, preferred_element_type=F32)
        both = both.astype(BF16)
        if k == 3:
            sent[...] = both
        else:
            other_rows[k][...] = both[:rows]
            mine_rows[k] = both[rows:]


def stack_kernel(a, b, out):
    rows = a.shape[0]
    out[:rows] = a[...]
    out[rows:] = b[...]


def add_kernel(a, b, out):
    rows = a.shape[0]
    out[:rows] = a[...] + b[:rows]
    out[rows:] = jnp.zeros((out.shape[0] - rows, out.shape[1]), BF16)


def last_rows_kernel(a, b, c, out):
    out[...] = a[...] + b[...] + c[: out.shape[0]]


def softmax_part(acc, targets):
    hit = hits(targets, acc.shape)
    top = jnp.max(acc, axis=1, keepdims=True)
    shifted = jnp.exp(acc - top)
    total = jnp.sum(shifted, axis=1, keepdims=True)
    label = jnp.sum(jnp.where(hit, acc, 0.0), axis=1, keepdims=True)
    return rows_of([top, total, label]), jnp.where(hit, 0.0, shifted).astype(BF16)


def own_kernel(place, kept, targets, a, b, c, d, stats, sums):
    acc = 0
    for k, shard in enumerate((a, b, c, d)):
        acc += jnp.dot(shard[...], block(kept, place, k, shard.shape[1]), preferred_element_type=F32)
    stats[...], others = softmax_part(acc, targets)
    for k in range(sums.shape[0]):
        weights = block(kept, place, k, sums.shape[2])
        sums[k] = lax.dot_general(others, weights, ROWS_BY_ROWS, preferred_element_type=F32)


def start_kernel(place, kept, a, bc, out):
    rows, width = a.shape
    acc = jnp.dot(a[...], block(kept, place, 0, width), preferred_element_type=F32)
    acc += jnp.dot(bc[:rows], block(kept, place, 1, width), preferred_element_type=F32)
    acc += jnp.dot(bc[rows:], block(kept, place, 2, width), preferred_element_type=F32)
    out[...] = acc


def peer_kernel(place, kept, targets, partial, d, block3, others):
    rows, width = d.shape
    acc = partial[...] + jnp.dot(d[...], block(kept, place, 3, width), preferred_element_type=F32)
    stats, shifted = softmax_part(acc, targets)
    block3[rows:] = with_tail(as_rows(stats), width)
    weights = block(kept, place, 3, width)
    block3[:rows] = lax.dot_general(shifted, weights, ROWS_BY_ROWS, preferred_element_type=F32).astype(BF16)
    others[...] = shifted


def rest_kernel(place, kept, others, block0, block21):
    rows, width = block0.shape
    for k, out in ((2, block21.at[:rows]), (1, block21.at[rows:]), (0, block0)):
        weights = block(kept, place, k, width)
        out[...] = lax.dot_general(others[...], weights, ROWS_BY_ROWS, preferred_element_type=F32).astype(BF16)


def join(a, b):
    top = jnp.maximum(a[0], b[0])
    return top, a[1] * jnp.exp(a[0] - top) + b[1] * jnp.exp(b[0] - top), a[2] + b[2]


def as_rows(a):
    return a[0:1], a[1:2], a[2:3]


def with_tail(stats, width):
    high = [row.astype(BF16).astype(F32) for row in stats]
    rest = [row - term for row, term in zip(stats, high)]
    middle = [row.astype(BF16).astype(F32) for row in rest]
    low = [row - term for row, term in zip(rest, middle)]
    rows = jnp.concatenate(high + middle + low + [jnp.zeros((7, stats[0].shape[1]), F32)], axis=0)
    return jnp.concatenate([rows, jnp.zeros((16, width - rows.shape[1]), F32)], axis=1).astype(BF16)


def from_tail(ref, rows):
    tail = ref[rows:].astype(F32)[:, :rows]
    return [tail[i : i + 1] + tail[i + 3 : i + 4] + tail[i + 6 : i + 7] for i in range(3)]


def pair_kernel(own_stats, got, sums, pair, sent):
    rows = own_stats.shape[1]
    theirs = from_tail(got, rows)
    mine = as_rows(own_stats[...])
    both = join(mine, theirs)
    stats = jnp.concatenate(list(both) + [mine[0], theirs[0]] + [jnp.zeros((3, rows), F32)], axis=0)
    pair[...] = stats
    near, far = columns_of([jnp.exp(mine[0] - both[0]), jnp.exp(theirs[0] - both[0])])
    sent[...] = (near * sums[3] + far * got[:rows].astype(F32)).astype(BF16)


def join_kernel(pair, got, out):
    rows = pair.shape[1]
    near = as_rows(got[...])
    both = join(as_rows(pair[...]), near)
    out[...] = jnp.concatenate(list(both) + [near[0], jnp.zeros((4, rows), F32)], axis=0)


def block_sum(by, sums, got, picked, k):
    return by[0] * sums[k] + by[1] * got[...].astype(F32) + by[3] * picked[k].astype(F32)


def scale_kernel(scale, pair, half, far, sums, got, relayed, picked, near_picked, loss, columns, second):
    rows = second.shape[0]
    top, total, label = join(as_rows(half[...]), as_rows(far[...]))
    loss[...] = jnp.log(total) + top - label
    weighted = scale[...] / total
    factors = [weighted * jnp.exp(a - top) for a in (pair[3:4], pair[4:5], half[3:4])]
    missing = scale[...] * (jnp.exp(label - top) / total - 1.0)
    by = columns_of(factors + [missing])
    for i, column in enumerate(by):
        columns[i] = jnp.broadcast_to(column, columns.shape[1:])
    here = block_sum(by, sums, got.at[:rows], picked, 2)
    here += by[2] * relayed[...].astype(F32) + by[3] * near_picked[rows:].astype(F32)
    second[...] = here.astype(BF16)


def first_kernel(columns, sums, got, picked, out):
    by = [columns[i][:, :1] for i in range(4)]
    rows = out.shape[0]
    out[...] = block_sum(by, sums, got.at[rows:], picked, 1).astype(BF16)


def second_kernel(columns, sums, got, picked, second, out):
    by = [columns[i][:, :1] for i in range(4)]
    out[...] = block_sum(by, sums, got, picked, 0) + second[...].astype(F32)


def last_kernel(place, columns, partial, first, theirs, loss, other_loss, out, row_loss):
    here = partial[...] + first[...].astype(F32) + columns[3][:, :1] * theirs[...].astype(F32)
    out[...] = here.astype(BF16)
    rows = out.shape[0]
    lower = place[5] == 0
    row_loss[:rows] = jnp.where(lower, loss[...], other_loss[...])[0]
    row_loss[rows:] = jnp.where(lower, other_loss[...], loss[...])[0]


def two_by_four(hidden, weight, targets, row_weight):
    tensors = lax.axis_size("tensor")
    px, tz = lax.axis_index("pipe"), lax.axis_index("tensor")
    rows, width = hidden.shape
    vocab_dev = weight.shape[1]

    def along(a, k):
        return lax.ppermute(a, "tensor", partners(tensors, k))

    def across(a):
        return lax.ppermute(a, "pipe", [(0, 1), (1, 0)])

    def after(a, b):
        return lax.optimization_barrier((a, b))[0]

    def call(kernel, outs, ins, *args, scratch=(), aliases=None):
        return pl.pallas_call(
            kernel,
            out_shape=outs,
            in_specs=ins,
            out_specs=jax.tree.map(lambda _: VMEM, outs),
            scratch_shapes=list(scratch),
            input_output_aliases=aliases or {},
            compiler_params=LIMIT,
        )(*args)

    def shape(*dims, dtype=F32):
        return jax.ShapeDtypeStruct(dims, dtype)

    place = [tz ^ k for k in range(tensors)] + [(px * tensors + tz) * vocab_dev, px, lax.axis_index("dp") % 2]
    place = jnp.stack(place).astype(jnp.int32)
    piece = shape(rows, width, dtype=BF16)
    two = shape(2 * rows, width, dtype=BF16)
    tailed = shape(rows + 16, width, dtype=BF16)
    wide = shape(rows, 128, dtype=jnp.int32)

    weight = pltpu.with_memory_space_constraint(weight, pltpu.HBM)
    dma = [pltpu.SemaphoreType.DMA]
    column_sums = shape(tensors, rows, width)

    kept = call(fetch_kernel, pltpu.VMEM(weight.shape, BF16), [SMEM, HBM], place, weight, scratch=dma)
    hidden = after(hidden, [kept])

    z2 = along(hidden, 2)
    z1 = along(hidden, 1)
    x0 = across(hidden)
    kept, mine, other, scale = call(
        targets_kernel,
        [pltpu.VMEM(weight.shape, BF16), wide, wide, shape(1, rows)],
        [SMEM, HBM, VMEM, VMEM, VMEM],
        place, weight, targets, row_weight, kept, scratch=dma, aliases={4: 0},
    )
    z3 = along(after(z2, [scale]), 1)
    x12 = across(call(stack_kernel, two, [VMEM] * 2, after(z1, [x0]), after(z2, [scale])))

    mine_rows, rows0, rows1, rows2, rows3 = call(
        pick_kernel, [shape(3, rows, width, dtype=BF16), piece, piece, piece, two], [SMEM] + [VMEM] * 3,
        after(place, [z2]), kept, mine, other,
    )
    x3 = across(after(z3, [rows3]))
    relayed_rows = along(after(rows3, [z3]), 1)

    own_stats, sums = call(
        own_kernel, [shape(8, rows), column_sums], [SMEM] + [VMEM] * 6, place, kept, mine, hidden, z1, z2, z3
    )
    partial = call(start_kernel, shape(rows, vocab_dev), [SMEM] + [VMEM] * 3, place, kept, x0, x12)
    block3, others = call(
        peer_kernel, [tailed, shape(rows, vocab_dev, dtype=BF16)], [SMEM] + [VMEM] * 4,
        place, kept, after(other, [own_stats, relayed_rows]), partial, x3,
    )

    far_rows = call(add_kernel, shape(rows + 32, width, dtype=BF16), [VMEM] * 2, rows2, relayed_rows)
    far_rows = along(far_rows, 2)
    got3 = across(block3)
    block0, block21 = call(rest_kernel, [piece, two], [SMEM] + [VMEM] * 2, place, kept, others)
    pair, relayed = call(pair_kernel, [shape(8, rows), piece], [VMEM] * 3, own_stats, got3, sums)
    near = along(pair, 1)
    relayed = along(relayed, 1)
    got21 = across(after(block21, [pair]))
    half = call(join_kernel, shape(8, rows), [VMEM] * 2, after(pair, [far_rows]), near)
    far = along(half, 2)
    loss, columns, second = call(
        scale_kernel,
        [shape(1, rows), shape(4, rows, 128), piece],
        [VMEM] * 9,
        scale, pair, half, far, sums, got21, relayed, mine_rows, relayed_rows,
    )
    near_rows = along(after(rows1, [half]), 1)
    second = along(second, 2)
    got0 = across(after(block0, [got21]))
    picked = call(last_rows_kernel, piece, [VMEM] * 3, after(rows0, [got21]), near_rows, far_rows)
    picked = across(picked)
    other_loss = across(loss)
    first = along(call(first_kernel, piece, [VMEM] * 4, columns, sums, got21, mine_rows), 1)
    total = call(second_kernel, shape(rows, width), [VMEM] * 5, columns, sums, got0, mine_rows, second)
    return call(
        last_kernel, [piece, shape(2 * rows)], [SMEM] + [VMEM] * 6,
        place, columns, total, first, picked, loss, other_loss,
    )


def per_device(hidden, weight, targets, row_weight):
    if lax.axis_size("pipe") == 2 and lax.axis_size("tensor") == 4:
        return two_by_four(hidden, weight, targets, row_weight)
    return any_mesh(hidden, weight, targets, row_weight)


def solution(mesh):
    in_specs = (P(("dp", "pipe"), "tensor"), P(None, ("pipe", "tensor")), P("dp"), P("dp"))
    out_specs = (P(("dp", "pipe"), "tensor"), P("dp"))
    return jax.shard_map(
        per_device, mesh=mesh, in_specs=in_specs, out_specs=out_specs, check_vma=False
    )
```

```python
import functools

import jax
import jax.numpy as jnp
from jax import lax
from jax.experimental import pallas as pl
from jax.experimental.pallas import tpu as pltpu
from jax.sharding import PartitionSpec as P

BF16, F32 = jnp.bfloat16, jnp.float32
ROWS_BY_ROWS = (((1,), (1,)), ((), ()))
VMEM = pl.BlockSpec(memory_space=pltpu.VMEM)
SMEM = pl.BlockSpec(memory_space=pltpu.SMEM)
HBM = pl.BlockSpec(memory_space=pltpu.HBM)
LIMIT = pltpu.CompilerParams(vmem_limit_bytes=24 * 2**20)


def partners(n, k):
    if n & (n - 1):
        return [(i, (i + k) % n) for i in range(n)]
    return [(i, i ^ k) for i in range(n)]


def source(me, n, k):
    if n & (n - 1):
        return lax.rem(me - k + n, n)
    return me ^ k


def target(me, n, k):
    if n & (n - 1):
        return lax.rem(me + k, n)
    return me ^ k


def merge(a, b):
    top = jnp.maximum(a[0], b[0])
    total = a[1] * jnp.exp(a[0] - top) + b[1] * jnp.exp(b[0] - top)
    return jnp.stack([top, total, a[2] + b[2]])


def any_mesh(hidden, weight, targets, row_weight):
    pipes, tensors = lax.axis_size("pipe"), lax.axis_size("tensor")
    px, tz = lax.axis_index("pipe"), lax.axis_index("tensor")
    rows, width = hidden.shape
    vocab_dev = weight.shape[1]
    offset = (px * tensors + tz) * vocab_dev

    w_in = [lax.dynamic_slice_in_dim(weight, source(tz, tensors, k) * width, width, 0) for k in range(tensors)]
    w_out = [lax.dynamic_slice_in_dim(weight, target(tz, tensors, k) * width, width, 0) for k in range(tensors)]

    def tensor_permute(a, k):
        return a if k == 0 else lax.ppermute(a, "tensor", partners(tensors, k))

    def pipe_permute(a, j):
        return a if j == 0 else lax.ppermute(a, "pipe", partners(pipes, j))

    local_targets = [targets.reshape(pipes, rows)[source(px, pipes, j)] for j in range(pipes)]
    local_scale = [row_weight.reshape(pipes, rows)[source(px, pipes, j)] for j in range(pipes)]
    columns = lax.broadcasted_iota(jnp.int32, (rows, vocab_dev), 1) + offset
    arrived = [tensor_permute(hidden, k) for k in range(tensors)]
    logits, stats = [], []
    for j in range(pipes):
        acc = 0
        for k in range(tensors):
            acc += jnp.dot(pipe_permute(arrived[k], j), w_in[k], preferred_element_type=F32)
        logits.append(acc)
        m = jnp.max(acc, axis=1)
        s = jnp.sum(jnp.exp(acc - m[:, None]), axis=1)
        label = jnp.sum(jnp.where(columns == local_targets[j][:, None], acc, 0.0), axis=1)
        stats.append(jnp.stack([m, s, label]))
    mine = jnp.stack(stats)
    whole = jnp.zeros_like(mine)
    for j in range(pipes):
        whole = whole.at[source(px, pipes, j)].set(mine[j])
    every = lax.all_gather(whole, "pipe")
    whole = every[0]
    for p in range(1, pipes):
        whole = jax.vmap(merge)(whole, every[p])
    total = whole
    for k in range(1, tensors):
        total = jax.vmap(merge)(total, tensor_permute(whole, k))
    row_loss = (jnp.log(total[:, 1]) + total[:, 0] - total[:, 2]).reshape(-1)
    dlogits = []
    for j in range(pipes):
        m, s, _ = total[source(px, pipes, j)]
        hit = (columns == local_targets[j][:, None]).astype(F32)
        scaled = jnp.exp(logits[j] - m[:, None]) / s[:, None] - hit
        dlogits.append((local_scale[j][:, None] * scaled).astype(BF16))
    sums = [None] * tensors
    for k in range(tensors - 1, -1, -1):
        acc = 0
        for j in range(pipes - 1, -1, -1):
            part = lax.dot_general(dlogits[j], w_out[k], ROWS_BY_ROWS, preferred_element_type=F32)
            if j:
                part = lax.ppermute(part.astype(BF16), "pipe", [(b, a) for a, b in partners(pipes, j)]).astype(F32)
            acc += part
        if k:
            acc = tensor_permute(acc.astype(BF16), k).astype(F32)
        sums[k] = acc
    return sum(sums[1:], sums[0]).astype(BF16), row_loss


def block(ref, place, k, width):
    return ref[pl.ds(pl.multiple_of(place[k] * width, width), width), :]


def columns_of(row_list):
    rows = row_list[0].shape[1]
    table = jnp.concatenate(row_list + [jnp.zeros((128 - len(row_list), rows), F32)], axis=0)
    table = jnp.transpose(table)
    return [table[:, i : i + 1] for i in range(len(row_list))]


def rows_of(columns):
    lane = lax.broadcasted_iota(jnp.int32, (columns[0].shape[0], 128), 1)
    wide = jnp.zeros(lane.shape, F32)
    for i, column in enumerate(columns):
        wide = jnp.where(lane == i, column, wide)
    return jnp.transpose(wide)[:8, :]


def hits(targets, shape):
    return lax.broadcasted_iota(jnp.int32, shape, 1) == targets[:, :1]


def fetch_kernel(place, weight, kept, sem):
    @pl.when(place[6] == 0)
    def _():
        copy = pltpu.make_async_copy(weight, kept, sem)
        copy.start()
        copy.wait()


def targets_kernel(place, weight, targets, scale, fetched, kept, mine, other, weights_of, sem):
    copy = pltpu.make_async_copy(weight, kept, sem)

    @pl.when(place[6] == 1)
    def _():
        copy.start()

    rows = mine.shape[0]
    lower = place[5] == 0
    targets, scale = targets[...].reshape(1, -1), scale[...].reshape(1, -1)
    halves = [(targets[:, :rows] - place[4]).astype(F32), (targets[:, rows:] - place[4]).astype(F32)]
    own = jnp.where(lower, halves[0], halves[1])
    theirs = jnp.where(lower, halves[1], halves[0])
    own, theirs = [column.astype(jnp.int32) for column in columns_of([own, theirs])]
    mine[...] = jnp.broadcast_to(own, mine.shape)
    other[...] = jnp.broadcast_to(theirs, other.shape)
    weights_of[...] = jnp.where(lower, scale[:, :rows], scale[:, rows:])

    @pl.when(place[6] == 1)
    def _():
        copy.wait()


def pick_kernel(place, kept, mine, other, mine_rows, other0, other1, other2, sent):
    rows, width = other0.shape
    other_rows = (other0, other1, other2)
    column = jnp.concatenate([other[:, :1], mine[:, :1]], axis=0)
    entry = lax.broadcasted_iota(jnp.int32, (2 * rows, kept.shape[1]), 1)
    one_hot = (entry == column).astype(F32).astype(BF16)
    for k in (3, 2, 1, 0):
        both = lax.dot_general(one_hot, block(kept, place, k, width), ROWS_BY_ROWS, preferred_element_type=F32)
        both = both.astype(BF16)
        if k == 3:
            sent[...] = both
        else:
            other_rows[k][...] = both[:rows]
            mine_rows[k] = both[rows:]


def stack_kernel(a, b, out):
    rows = a.shape[0]
    out[:rows] = a[...]
    out[rows:] = b[...]


def add_kernel(a, b, out):
    rows = a.shape[0]
    out[:rows] = a[...] + b[:rows]
    out[rows:] = jnp.zeros((out.shape[0] - rows, out.shape[1]), BF16)


def last_rows_kernel(a, b, c, out):
    out[...] = a[...] + b[...] + c[: out.shape[0]]


def softmax_part(acc, targets):
    hit = hits(targets, acc.shape)
    top = jnp.max(acc, axis=1, keepdims=True)
    shifted = jnp.exp(acc - top)
    total = jnp.sum(shifted, axis=1, keepdims=True)
    label = jnp.sum(jnp.where(hit, acc, 0.0), axis=1, keepdims=True)
    return rows_of([top, total, label]), jnp.where(hit, 0.0, shifted).astype(BF16)


def own_kernel(place, kept, targets, a, b, c, d, stats, sums):
    acc = 0
    for k, shard in enumerate((a, b, c, d)):
        acc += jnp.dot(shard[...], block(kept, place, k, shard.shape[1]), preferred_element_type=F32)
    stats[...], others = softmax_part(acc, targets)
    for k in range(sums.shape[0]):
        weights = block(kept, place, k, sums.shape[2])
        sums[k] = lax.dot_general(others, weights, ROWS_BY_ROWS, preferred_element_type=F32)


def start_kernel(place, kept, a, bc, out):
    rows, width = a.shape
    acc = jnp.dot(a[...], block(kept, place, 0, width), preferred_element_type=F32)
    acc += jnp.dot(bc[:rows], block(kept, place, 1, width), preferred_element_type=F32)
    acc += jnp.dot(bc[rows:], block(kept, place, 2, width), preferred_element_type=F32)
    out[...] = acc


def peer_kernel(place, kept, targets, partial, d, block3, others):
    rows, width = d.shape
    acc = partial[...] + jnp.dot(d[...], block(kept, place, 3, width), preferred_element_type=F32)
    stats, shifted = softmax_part(acc, targets)
    block3[rows:] = with_tail(as_rows(stats), width)
    weights = block(kept, place, 3, width)
    block3[:rows] = lax.dot_general(shifted, weights, ROWS_BY_ROWS, preferred_element_type=F32).astype(BF16)
    others[...] = shifted


def rest_kernel(ks, place, kept, others, blocks):
    rows, width = others.shape[0], blocks.shape[1]
    for i, k in enumerate(ks):
        out = blocks.at[i * rows : (i + 1) * rows]
        weights = block(kept, place, k, width)
        out[...] = lax.dot_general(others[...], weights, ROWS_BY_ROWS, preferred_element_type=F32).astype(BF16)


def join(a, b):
    top = jnp.maximum(a[0], b[0])
    return top, a[1] * jnp.exp(a[0] - top) + b[1] * jnp.exp(b[0] - top), a[2] + b[2]


def as_rows(a):
    return a[0:1], a[1:2], a[2:3]


def with_tail(stats, width):
    high = [row.astype(BF16).astype(F32) for row in stats]
    rest = [row - term for row, term in zip(stats, high)]
    middle = [row.astype(BF16).astype(F32) for row in rest]
    low = [row - term for row, term in zip(rest, middle)]
    rows = jnp.concatenate(high + middle + low + [jnp.zeros((7, stats[0].shape[1]), F32)], axis=0)
    return jnp.concatenate([rows, jnp.zeros((16, width - rows.shape[1]), F32)], axis=1).astype(BF16)


def from_tail(ref, rows):
    tail = ref[rows:].astype(F32)[:, :rows]
    return [tail[i : i + 1] + tail[i + 3 : i + 4] + tail[i + 6 : i + 7] for i in range(3)]


def pair_kernel(own_stats, got, sums, pair, sent):
    rows = own_stats.shape[1]
    theirs = from_tail(got, rows)
    mine = as_rows(own_stats[...])
    both = join(mine, theirs)
    stats = jnp.concatenate(list(both) + [mine[0], theirs[0]] + [jnp.zeros((3, rows), F32)], axis=0)
    pair[...] = stats
    near, far = columns_of([jnp.exp(mine[0] - both[0]), jnp.exp(theirs[0] - both[0])])
    sent[...] = (near * sums[3] + far * got[:rows].astype(F32)).astype(BF16)


def join_kernel(pair, got, out):
    rows = pair.shape[1]
    near = as_rows(got[...])
    both = join(as_rows(pair[...]), near)
    out[...] = jnp.concatenate(list(both) + [near[0], jnp.zeros((4, rows), F32)], axis=0)


def block_sum(by, sums, got, picked, k):
    return by[0] * sums[k] + by[1] * got[...].astype(F32) + by[3] * picked[k].astype(F32)


def scale_kernel(scale, pair, half, far, sums, got, relayed, picked, near_picked, loss, columns, second, first):
    rows = second.shape[0]
    top, total, label = join(as_rows(half[...]), as_rows(far[...]))
    loss[...] = jnp.log(total) + top - label
    weighted = scale[...] / total
    factors = [weighted * jnp.exp(a - top) for a in (pair[3:4], pair[4:5], half[3:4])]
    missing = scale[...] * (jnp.exp(label - top) / total - 1.0)
    by = columns_of(factors + [missing])
    for i, column in enumerate(by):
        columns[i] = jnp.broadcast_to(column, columns.shape[1:])
    here = block_sum(by, sums, got.at[:rows], picked, 2)
    here += by[2] * relayed[...].astype(F32) + by[3] * near_picked[rows:].astype(F32)
    second[...] = here.astype(BF16)
    first[...] = block_sum(by, sums, got.at[rows:], picked, 1).astype(BF16)


def second_kernel(columns, sums, got, picked, second, out):
    by = [columns[i][:, :1] for i in range(4)]
    out[...] = block_sum(by, sums, got, picked, 0) + second[...].astype(F32)


def last_kernel(place, columns, partial, first, theirs, loss, other_loss, out, row_loss):
    here = partial[...] + first[...].astype(F32) + columns[3][:, :1] * theirs[...].astype(F32)
    out[...] = here.astype(BF16)
    rows = out.shape[0]
    lower = place[5] == 0
    row_loss[:rows] = jnp.where(lower, loss[...], other_loss[...])[0]
    row_loss[rows:] = jnp.where(lower, other_loss[...], loss[...])[0]


def two_by_four(hidden, weight, targets, row_weight):
    tensors = lax.axis_size("tensor")
    px, tz = lax.axis_index("pipe"), lax.axis_index("tensor")
    rows, width = hidden.shape
    vocab_dev = weight.shape[1]

    def along(a, k):
        return lax.ppermute(a, "tensor", partners(tensors, k))

    def across(a):
        return lax.ppermute(a, "pipe", [(0, 1), (1, 0)])

    def after(a, b):
        return lax.optimization_barrier((a, b))[0]

    def call(kernel, outs, ins, *args, scratch=(), aliases=None):
        return pl.pallas_call(
            kernel,
            out_shape=outs,
            in_specs=ins,
            out_specs=jax.tree.map(lambda _: VMEM, outs),
            scratch_shapes=list(scratch),
            input_output_aliases=aliases or {},
            compiler_params=LIMIT,
        )(*args)

    def shape(*dims, dtype=F32):
        return jax.ShapeDtypeStruct(dims, dtype)

    place = [tz ^ k for k in range(tensors)] + [(px * tensors + tz) * vocab_dev, px, lax.axis_index("dp") % 2]
    place = jnp.stack(place).astype(jnp.int32)
    piece = shape(rows, width, dtype=BF16)
    two = shape(2 * rows, width, dtype=BF16)
    tailed = shape(rows + 16, width, dtype=BF16)
    wide = shape(rows, 128, dtype=jnp.int32)

    weight = pltpu.with_memory_space_constraint(weight, pltpu.HBM)
    dma = [pltpu.SemaphoreType.DMA]
    column_sums = shape(tensors, rows, width)

    kept = call(fetch_kernel, pltpu.VMEM(weight.shape, BF16), [SMEM, HBM], place, weight, scratch=dma)
    hidden = after(hidden, [kept])

    z2 = along(hidden, 2)
    z1 = along(hidden, 1)
    x0 = across(hidden)
    kept, mine, other, scale = call(
        targets_kernel,
        [pltpu.VMEM(weight.shape, BF16), wide, wide, shape(1, rows)],
        [SMEM, HBM, VMEM, VMEM, VMEM],
        place, weight, targets, row_weight, kept, scratch=dma, aliases={4: 0},
    )
    z3 = along(after(z2, [scale]), 1)
    x12 = across(call(stack_kernel, two, [VMEM] * 2, after(z1, [x0]), after(z2, [scale])))

    mine_rows, rows0, rows1, rows2, rows3 = call(
        pick_kernel, [shape(3, rows, width, dtype=BF16), piece, piece, piece, two], [SMEM] + [VMEM] * 3,
        after(place, [z2]), kept, mine, other,
    )
    x3 = across(after(z3, [rows3]))
    relayed_rows = along(after(rows3, [z3]), 1)

    own_stats, sums = call(
        own_kernel, [shape(8, rows), column_sums], [SMEM] + [VMEM] * 6, place, kept, mine, hidden, z1, z2, z3
    )
    partial = call(start_kernel, shape(rows, vocab_dev), [SMEM] + [VMEM] * 3, place, kept, x0, x12)
    block3, others = call(
        peer_kernel, [tailed, shape(rows, vocab_dev, dtype=BF16)], [SMEM] + [VMEM] * 4,
        place, kept, after(other, [own_stats, relayed_rows]), partial, x3,
    )

    far_rows = call(add_kernel, shape(rows + 32, width, dtype=BF16), [VMEM] * 2, rows2, relayed_rows)
    far_rows = along(far_rows, 2)
    got3 = across(block3)
    block21 = call(functools.partial(rest_kernel, (2, 1)), two, [SMEM] + [VMEM] * 2, place, kept, others)
    pair, relayed = call(pair_kernel, [shape(8, rows), piece], [VMEM] * 3, own_stats, got3, sums)
    near = along(pair, 1)
    relayed = along(relayed, 1)
    got21 = across(after(block21, [pair]))
    block0 = call(
        functools.partial(rest_kernel, (0,)), piece, [SMEM] + [VMEM] * 2, after(place, [pair]), kept, others
    )
    half = call(join_kernel, shape(8, rows), [VMEM] * 2, after(pair, [far_rows]), near)
    far = along(half, 2)
    loss, columns, second, first = call(
        scale_kernel,
        [shape(1, rows), shape(4, rows, 128), piece, piece],
        [VMEM] * 9,
        scale, pair, half, far, sums, got21, relayed, mine_rows, relayed_rows,
    )
    near_rows = along(after(rows1, [half]), 1)
    second = along(second, 2)
    first = along(first, 1)
    got0 = across(after(block0, [got21]))
    picked = call(last_rows_kernel, piece, [VMEM] * 3, after(rows0, [got21]), near_rows, far_rows)
    picked = across(picked)
    other_loss = across(loss)
    total = call(second_kernel, shape(rows, width), [VMEM] * 5, columns, sums, got0, mine_rows, second)
    return call(
        last_kernel, [piece, shape(2 * rows)], [SMEM] + [VMEM] * 6,
        place, columns, total, first, picked, loss, other_loss,
    )


def per_device(hidden, weight, targets, row_weight):
    if lax.axis_size("pipe") == 2 and lax.axis_size("tensor") == 4:
        return two_by_four(hidden, weight, targets, row_weight)
    return any_mesh(hidden, weight, targets, row_weight)


def solution(mesh):
    in_specs = (P(("dp", "pipe"), "tensor"), P(None, ("pipe", "tensor")), P("dp"), P("dp"))
    out_specs = (P(("dp", "pipe"), "tensor"), P("dp"))
    return jax.shard_map(
        per_device, mesh=mesh, in_specs=in_specs, out_specs=out_specs, check_vma=False
    )
```

```python
import functools

import jax
import jax.numpy as jnp
from jax import lax
from jax.experimental import pallas as pl
from jax.experimental.pallas import tpu as pltpu
from jax.sharding import PartitionSpec as P

BF16, F32 = jnp.bfloat16, jnp.float32
ROWS_BY_ROWS = (((1,), (1,)), ((), ()))
VMEM = pl.BlockSpec(memory_space=pltpu.VMEM)
SMEM = pl.BlockSpec(memory_space=pltpu.SMEM)
HBM = pl.BlockSpec(memory_space=pltpu.HBM)
LIMIT = pltpu.CompilerParams(vmem_limit_bytes=24 * 2**20)


def partners(n, k):
    if n & (n - 1):
        return [(i, (i + k) % n) for i in range(n)]
    return [(i, i ^ k) for i in range(n)]


def source(me, n, k):
    if n & (n - 1):
        return lax.rem(me - k + n, n)
    return me ^ k


def target(me, n, k):
    if n & (n - 1):
        return lax.rem(me + k, n)
    return me ^ k


def merge(a, b):
    top = jnp.maximum(a[0], b[0])
    total = a[1] * jnp.exp(a[0] - top) + b[1] * jnp.exp(b[0] - top)
    return jnp.stack([top, total, a[2] + b[2]])


def any_mesh(hidden, weight, targets, row_weight):
    pipes, tensors = lax.axis_size("pipe"), lax.axis_size("tensor")
    px, tz = lax.axis_index("pipe"), lax.axis_index("tensor")
    rows, width = hidden.shape
    vocab_dev = weight.shape[1]
    offset = (px * tensors + tz) * vocab_dev

    w_in = [lax.dynamic_slice_in_dim(weight, source(tz, tensors, k) * width, width, 0) for k in range(tensors)]
    w_out = [lax.dynamic_slice_in_dim(weight, target(tz, tensors, k) * width, width, 0) for k in range(tensors)]

    def tensor_permute(a, k):
        return a if k == 0 else lax.ppermute(a, "tensor", partners(tensors, k))

    def pipe_permute(a, j):
        return a if j == 0 else lax.ppermute(a, "pipe", partners(pipes, j))

    local_targets = [targets.reshape(pipes, rows)[source(px, pipes, j)] for j in range(pipes)]
    local_scale = [row_weight.reshape(pipes, rows)[source(px, pipes, j)] for j in range(pipes)]
    columns = lax.broadcasted_iota(jnp.int32, (rows, vocab_dev), 1) + offset
    arrived = [tensor_permute(hidden, k) for k in range(tensors)]
    logits, stats = [], []
    for j in range(pipes):
        acc = 0
        for k in range(tensors):
            acc += jnp.dot(pipe_permute(arrived[k], j), w_in[k], preferred_element_type=F32)
        logits.append(acc)
        m = jnp.max(acc, axis=1)
        s = jnp.sum(jnp.exp(acc - m[:, None]), axis=1)
        label = jnp.sum(jnp.where(columns == local_targets[j][:, None], acc, 0.0), axis=1)
        stats.append(jnp.stack([m, s, label]))
    mine = jnp.stack(stats)
    whole = jnp.zeros_like(mine)
    for j in range(pipes):
        whole = whole.at[source(px, pipes, j)].set(mine[j])
    every = lax.all_gather(whole, "pipe")
    whole = every[0]
    for p in range(1, pipes):
        whole = jax.vmap(merge)(whole, every[p])
    total = whole
    for k in range(1, tensors):
        total = jax.vmap(merge)(total, tensor_permute(whole, k))
    row_loss = (jnp.log(total[:, 1]) + total[:, 0] - total[:, 2]).reshape(-1)
    dlogits = []
    for j in range(pipes):
        m, s, _ = total[source(px, pipes, j)]
        hit = (columns == local_targets[j][:, None]).astype(F32)
        scaled = jnp.exp(logits[j] - m[:, None]) / s[:, None] - hit
        dlogits.append((local_scale[j][:, None] * scaled).astype(BF16))
    sums = [None] * tensors
    for k in range(tensors - 1, -1, -1):
        acc = 0
        for j in range(pipes - 1, -1, -1):
            part = lax.dot_general(dlogits[j], w_out[k], ROWS_BY_ROWS, preferred_element_type=F32)
            if j:
                part = lax.ppermute(part.astype(BF16), "pipe", [(b, a) for a, b in partners(pipes, j)]).astype(F32)
            acc += part
        if k:
            acc = tensor_permute(acc.astype(BF16), k).astype(F32)
        sums[k] = acc
    return sum(sums[1:], sums[0]).astype(BF16), row_loss


def block(ref, place, k, width):
    return ref[pl.ds(pl.multiple_of(place[k] * width, width), width), :]


def columns_of(row_list):
    rows = row_list[0].shape[1]
    table = jnp.concatenate(row_list + [jnp.zeros((128 - len(row_list), rows), F32)], axis=0)
    table = jnp.transpose(table)
    return [table[:, i : i + 1] for i in range(len(row_list))]


def rows_of(columns):
    lane = lax.broadcasted_iota(jnp.int32, (columns[0].shape[0], 128), 1)
    wide = jnp.zeros(lane.shape, F32)
    for i, column in enumerate(columns):
        wide = jnp.where(lane == i, column, wide)
    return jnp.transpose(wide)[:8, :]


def hits(targets, shape):
    return lax.broadcasted_iota(jnp.int32, shape, 1) == targets[:, :1]


def fetch_kernel(place, weight, kept, sem):
    @pl.when(place[6] == 0)
    def _():
        copy = pltpu.make_async_copy(weight, kept, sem)
        copy.start()
        copy.wait()


def targets_kernel(place, weight, targets, scale, fetched, kept, mine, other, weights_of, sem):
    copy = pltpu.make_async_copy(weight, kept, sem)

    @pl.when(place[6] == 1)
    def _():
        copy.start()

    rows = mine.shape[0]
    lower = place[5] == 0
    targets, scale = targets[...].reshape(1, -1), scale[...].reshape(1, -1)
    halves = [(targets[:, :rows] - place[4]).astype(F32), (targets[:, rows:] - place[4]).astype(F32)]
    own = jnp.where(lower, halves[0], halves[1])
    theirs = jnp.where(lower, halves[1], halves[0])
    own, theirs = [column.astype(jnp.int32) for column in columns_of([own, theirs])]
    mine[...] = jnp.broadcast_to(own, mine.shape)
    other[...] = jnp.broadcast_to(theirs, other.shape)
    weights_of[...] = jnp.where(lower, scale[:, :rows], scale[:, rows:])

    @pl.when(place[6] == 1)
    def _():
        copy.wait()


def pick_kernel(place, kept, mine, other, mine_rows, other0, other1, other2, sent):
    rows, width = other0.shape
    other_rows = (other0, other1, other2)
    column = jnp.concatenate([other[:, :1], mine[:, :1]], axis=0)
    entry = lax.broadcasted_iota(jnp.int32, (2 * rows, kept.shape[1]), 1)
    one_hot = (entry == column).astype(F32).astype(BF16)
    for k in (3, 2, 1, 0):
        both = lax.dot_general(one_hot, block(kept, place, k, width), ROWS_BY_ROWS, preferred_element_type=F32)
        both = both.astype(BF16)
        if k == 3:
            sent[...] = both
        else:
            other_rows[k][...] = both[:rows]
            mine_rows[k] = both[rows:]


def stack_kernel(a, b, out):
    rows = a.shape[0]
    out[:rows] = a[...]
    out[rows:] = b[...]


def add_kernel(a, b, out):
    rows = a.shape[0]
    out[:rows] = a[...] + b[:rows]
    out[rows:] = jnp.zeros((out.shape[0] - rows, out.shape[1]), BF16)


def last_rows_kernel(a, b, c, out):
    out[...] = a[...] + b[...] + c[: out.shape[0]]


def softmax_part(acc, targets):
    hit = hits(targets, acc.shape)
    top = jnp.max(acc, axis=1, keepdims=True)
    shifted = jnp.exp(acc - top)
    total = jnp.sum(shifted, axis=1, keepdims=True)
    label = jnp.sum(jnp.where(hit, acc, 0.0), axis=1, keepdims=True)
    return rows_of([top, total, label]), jnp.where(hit, 0.0, shifted).astype(BF16)


def own_kernel(place, kept, targets, a, b, c, d, stats, sums):
    acc = 0
    for k, shard in enumerate((a, b, c, d)):
        acc += jnp.dot(shard[...], block(kept, place, k, shard.shape[1]), preferred_element_type=F32)
    stats[...], others = softmax_part(acc, targets)
    for k in range(sums.shape[0]):
        weights = block(kept, place, k, sums.shape[2])
        sums[k] = lax.dot_general(others, weights, ROWS_BY_ROWS, preferred_element_type=F32)


def start_kernel(place, kept, a, bc, out):
    rows, width = a.shape
    acc = jnp.dot(a[...], block(kept, place, 0, width), preferred_element_type=F32)
    acc += jnp.dot(bc[:rows], block(kept, place, 1, width), preferred_element_type=F32)
    acc += jnp.dot(bc[rows:], block(kept, place, 2, width), preferred_element_type=F32)
    out[...] = acc


def peer_kernel(place, kept, targets, partial, d, block3, others):
    rows, width = d.shape
    acc = partial[...] + jnp.dot(d[...], block(kept, place, 3, width), preferred_element_type=F32)
    stats, shifted = softmax_part(acc, targets)
    block3[rows:] = with_tail(as_rows(stats), width)
    weights = block(kept, place, 3, width)
    block3[:rows] = lax.dot_general(shifted, weights, ROWS_BY_ROWS, preferred_element_type=F32).astype(BF16)
    others[...] = shifted


def rest_kernel(ks, place, kept, others, blocks):
    rows, width = others.shape[0], blocks.shape[1]
    for i, k in enumerate(ks):
        out = blocks.at[i * rows : (i + 1) * rows]
        weights = block(kept, place, k, width)
        out[...] = lax.dot_general(others[...], weights, ROWS_BY_ROWS, preferred_element_type=F32).astype(BF16)


def join(a, b):
    top = jnp.maximum(a[0], b[0])
    return top, a[1] * jnp.exp(a[0] - top) + b[1] * jnp.exp(b[0] - top), a[2] + b[2]


def as_rows(a):
    return a[0:1], a[1:2], a[2:3]


def with_tail(stats, width):
    high = [row.astype(BF16).astype(F32) for row in stats]
    rest = [row - term for row, term in zip(stats, high)]
    middle = [row.astype(BF16).astype(F32) for row in rest]
    low = [row - term for row, term in zip(rest, middle)]
    rows = jnp.concatenate(high + middle + low + [jnp.zeros((7, stats[0].shape[1]), F32)], axis=0)
    return jnp.concatenate([rows, jnp.zeros((16, width - rows.shape[1]), F32)], axis=1).astype(BF16)


def from_tail(ref, rows):
    tail = ref[rows:].astype(F32)[:, :rows]
    return [tail[i : i + 1] + tail[i + 3 : i + 4] + tail[i + 6 : i + 7] for i in range(3)]


def pair_kernel(own_stats, got, sums, pair, sent):
    rows = own_stats.shape[1]
    theirs = from_tail(got, rows)
    mine = as_rows(own_stats[...])
    both = join(mine, theirs)
    stats = jnp.concatenate(list(both) + [mine[0], theirs[0]] + [jnp.zeros((3, rows), F32)], axis=0)
    pair[...] = stats
    near, far = columns_of([jnp.exp(mine[0] - both[0]), jnp.exp(theirs[0] - both[0])])
    sent[...] = (near * sums[3] + far * got[:rows].astype(F32)).astype(BF16)


def join_kernel(pair, got, out):
    rows = pair.shape[1]
    near = as_rows(got[...])
    both = join(as_rows(pair[...]), near)
    out[...] = jnp.concatenate(list(both) + [near[0], jnp.zeros((4, rows), F32)], axis=0)


def block_sum(by, sums, got, picked, k):
    return by[0] * sums[k] + by[1] * got[...].astype(F32) + by[3] * picked[k].astype(F32)


def scale_kernel(scale, pair, half, far, sums, got, relayed, picked, near_picked, loss, columns, second, first):
    rows = second.shape[0]
    top, total, label = join(as_rows(half[...]), as_rows(far[...]))
    loss[...] = jnp.log(total) + top - label
    weighted = scale[...] / total
    factors = [weighted * jnp.exp(a - top) for a in (pair[3:4], pair[4:5], half[3:4])]
    missing = scale[...] * (jnp.exp(label - top) / total - 1.0)
    by = columns_of(factors + [missing])
    for i, column in enumerate(by):
        columns[i] = jnp.broadcast_to(column, columns.shape[1:])
    here = block_sum(by, sums, got.at[:rows], picked, 2)
    here += by[2] * relayed[...].astype(F32) + by[3] * near_picked[rows:].astype(F32)
    second[...] = here.astype(BF16)
    first[...] = block_sum(by, sums, got.at[rows:], picked, 1).astype(BF16)


def second_kernel(place, columns, sums, got, picked, second, loss, other_loss, out, row_loss):
    by = [columns[i][:, :1] for i in range(4)]
    out[...] = block_sum(by, sums, got, picked, 0) + second[...].astype(F32)
    rows = out.shape[0]
    lower = place[5] == 0
    row_loss[:rows] = jnp.where(lower, loss[...], other_loss[...])[0]
    row_loss[rows:] = jnp.where(lower, other_loss[...], loss[...])[0]


def last_kernel(columns, partial, first, theirs, out):
    here = partial[...] + first[...].astype(F32) + columns[3][:, :1] * theirs[...].astype(F32)
    out[...] = here.astype(BF16)


def two_by_four(hidden, weight, targets, row_weight):
    tensors = lax.axis_size("tensor")
    px, tz = lax.axis_index("pipe"), lax.axis_index("tensor")
    rows, width = hidden.shape
    vocab_dev = weight.shape[1]

    def along(a, k):
        return lax.ppermute(a, "tensor", partners(tensors, k))

    def across(a):
        return lax.ppermute(a, "pipe", [(0, 1), (1, 0)])

    def after(a, b):
        return lax.optimization_barrier((a, b))[0]

    def call(kernel, outs, ins, *args, scratch=(), aliases=None):
        return pl.pallas_call(
            kernel,
            out_shape=outs,
            in_specs=ins,
            out_specs=jax.tree.map(lambda _: VMEM, outs),
            scratch_shapes=list(scratch),
            input_output_aliases=aliases or {},
            compiler_params=LIMIT,
        )(*args)

    def shape(*dims, dtype=F32):
        return jax.ShapeDtypeStruct(dims, dtype)

    place = [tz ^ k for k in range(tensors)] + [(px * tensors + tz) * vocab_dev, px, lax.axis_index("dp") % 2]
    place = jnp.stack(place).astype(jnp.int32)
    piece = shape(rows, width, dtype=BF16)
    two = shape(2 * rows, width, dtype=BF16)
    tailed = shape(rows + 16, width, dtype=BF16)
    wide = shape(rows, 128, dtype=jnp.int32)

    weight = pltpu.with_memory_space_constraint(weight, pltpu.HBM)
    dma = [pltpu.SemaphoreType.DMA]
    column_sums = shape(tensors, rows, width)

    kept = call(fetch_kernel, pltpu.VMEM(weight.shape, BF16), [SMEM, HBM], place, weight, scratch=dma)
    hidden = after(hidden, [kept])

    z2 = along(hidden, 2)
    z1 = along(hidden, 1)
    x0 = across(hidden)
    kept, mine, other, scale = call(
        targets_kernel,
        [pltpu.VMEM(weight.shape, BF16), wide, wide, shape(1, rows)],
        [SMEM, HBM, VMEM, VMEM, VMEM],
        place, weight, targets, row_weight, kept, scratch=dma, aliases={4: 0},
    )
    z3 = along(after(z2, [scale]), 1)
    x12 = across(call(stack_kernel, two, [VMEM] * 2, after(z1, [x0]), after(z2, [scale])))

    mine_rows, rows0, rows1, rows2, rows3 = call(
        pick_kernel, [shape(3, rows, width, dtype=BF16), piece, piece, piece, two], [SMEM] + [VMEM] * 3,
        after(place, [z2]), kept, mine, other,
    )
    x3 = across(after(z3, [rows3]))
    relayed_rows = along(after(rows3, [z3]), 1)

    own_stats, sums = call(
        own_kernel, [shape(8, rows), column_sums], [SMEM] + [VMEM] * 6, place, kept, mine, hidden, z1, z2, z3
    )
    partial = call(start_kernel, shape(rows, vocab_dev), [SMEM] + [VMEM] * 3, place, kept, x0, x12)
    block3, others = call(
        peer_kernel, [tailed, shape(rows, vocab_dev, dtype=BF16)], [SMEM] + [VMEM] * 4,
        place, kept, after(other, [own_stats, relayed_rows]), partial, x3,
    )

    far_rows = call(add_kernel, shape(rows + 32, width, dtype=BF16), [VMEM] * 2, rows2, relayed_rows)
    far_rows = along(far_rows, 2)
    got3 = across(block3)
    block21 = call(functools.partial(rest_kernel, (2, 1)), two, [SMEM] + [VMEM] * 2, place, kept, others)
    pair, relayed = call(pair_kernel, [shape(8, rows), piece], [VMEM] * 3, own_stats, got3, sums)
    near = along(pair, 1)
    relayed = along(relayed, 1)
    got21 = across(after(block21, [pair]))
    block0 = call(
        functools.partial(rest_kernel, (0,)), piece, [SMEM] + [VMEM] * 2, after(place, [pair]), kept, others
    )
    half = call(join_kernel, shape(8, rows), [VMEM] * 2, after(pair, [far_rows]), near)
    far = along(half, 2)
    loss, columns, second, first = call(
        scale_kernel,
        [shape(1, rows), shape(4, rows, 128), piece, piece],
        [VMEM] * 9,
        scale, pair, half, far, sums, got21, relayed, mine_rows, relayed_rows,
    )
    near_rows = along(after(rows1, [half]), 1)
    second = along(second, 2)
    first = along(first, 1)
    got0 = across(after(block0, [got21]))
    picked = call(last_rows_kernel, piece, [VMEM] * 3, after(rows0, [got21]), near_rows, far_rows)
    picked = across(picked)
    other_loss = across(loss)
    total, row_loss = call(
        second_kernel, [shape(rows, width), shape(2 * rows)], [SMEM] + [VMEM] * 7,
        place, columns, sums, got0, mine_rows, second, loss, other_loss,
    )
    return call(last_kernel, piece, [VMEM] * 4, columns, total, first, picked), row_loss


def per_device(hidden, weight, targets, row_weight):
    if lax.axis_size("pipe") == 2 and lax.axis_size("tensor") == 4:
        return two_by_four(hidden, weight, targets, row_weight)
    return any_mesh(hidden, weight, targets, row_weight)


def solution(mesh):
    in_specs = (P(("dp", "pipe"), "tensor"), P(None, ("pipe", "tensor")), P("dp"), P("dp"))
    out_specs = (P(("dp", "pipe"), "tensor"), P("dp"))
    return jax.shard_map(
        per_device, mesh=mesh, in_specs=in_specs, out_specs=out_specs, check_vma=False
    )
```
